128 devices in a mesh: row: 8 (over x, core), col: 16 (over y, z).
Axes of the slice: x: 4, y: 4, z: 4, core: 2. Of those that a mesh axis runs over, the one named last changes fastest.
Arguments:
- query_single: bfloat16 [1024, 384], P('row', 'col'), may hold values from -18 to 18
- query_rotation: float32 [9, 1024], P(None, 'row'), may hold values from -1 to 1, as said below
- query_anchor: float32 [3, 1024], P(None, 'row'), may hold values from -5 to 5
- query_chain: int32 [1024], P('row'), may hold values from 0 to 15, never falling along the last dimension, each value on 1 to 128 neighbouring positions
- key_single: bfloat16 [8192, 384], P(('col', 'row')), may hold values from -5 to 5
- key_rotation: float32 [9, 8192], P(None, ('col', 'row')), may hold values from -1 to 1, as said below
- key_anchor: float32 [3, 8192], P(None, ('col', 'row')), may hold values from -5 to 5
- key_chain: int32 [8192], P('col'), may hold values from 0 to 15, never falling along the last dimension, each value on 1 to 1024 neighbouring positions
- key_mask: int32 [8192], P('col'), may hold values 0 or 1
- pair_tile: bfloat16 [1024, 8192, 128], P('row', 'col'), may hold values from -50 to 50
- query_weight: bfloat16 [384, 192], replicated, may hold values from -0.3125 to 0.3125
- query_point_weight: bfloat16 [384, 144], replicated, may hold values from -0.3125 to 0.3125
- key_weight: bfloat16 [384, 192], replicated, may hold values from -0.3125 to 0.3125
- value_weight: bfloat16 [384, 192], replicated, may hold values from -0.3125 to 0.3125
- key_point_weight: bfloat16 [384, 144], replicated, may hold values from -0.3125 to 0.3125
- value_point_weight: bfloat16 [384, 288], replicated, may hold values from -0.3125 to 0.3125
- pair_weight: bfloat16 [128, 12], replicated, may hold values from -1 to 1
- head_gamma: float32 [12], replicated, may hold values from 0.05 to 1
- chain_gap: float32 [12], replicated, may hold values from -3 to 3
- out_weight: bfloat16 [2016, 384], P(None, 'col'), may hold values from -1 to 1
- norm_gain: float32 [384], P('col'), may hold values from 0.1 to 1.9
- norm_shift: float32 [384], P('col'), may hold values from -3 to 3
Outputs:
- updated_single: bfloat16 [1024, 384], P('row', 'col')
The draws below stay inside these ranges and needn't reach their ends.
Inputs may be any that keep to these rules, and one draw needn't show every extreme that they name: `query_rotation`: each column of 9 is a rotation matrix. `key_rotation`: each column of 9 is a rotation matrix. `query_chain`: ids never fall along the query residues. `key_chain`: ids never fall along the residues.
All inputs are finite; a program needn't handle non-finite values. No bound on the sum of `key_mask` on one device may be relied on, other than what follows from the above.
Results may differ from the reference program's by a relative error of at most 0.0095.
Values may be sent and summed in bfloat16 or wider, within the bound.
No kernel may reach another device: no remote copies, remote signals or barrier semaphores. Data moves between devices by JAX's collectives and lax.ppermute only.
A program may use at most 128 MiB of HBM per device.

```python
import math
import jax
import jax.numpy as jnp
import numpy as np
from jax import lax

D = 384
H = 12
C = 16
PQ = 4
PV = 8
CZ = 128
Q_DEV = 128
K_DEV = 512
CHAINS = 16
QUERIES = 1024
KEYS = 8192
FEAT = 168
OUT_FEAT = 2016


def rotation_table(key, residue_count):
    parts = jnp.clip(jax.random.normal(key, (4, residue_count), jnp.float32), -4.0, 4.0)
    leading = jax.random.uniform(jax.random.fold_in(key, 5), (residue_count,), jnp.float32, 0.4, 1.6)
    quat = jnp.concatenate([leading[None], parts[1:]], axis=0)
    unit = quat / jnp.sqrt(jnp.sum(quat * quat, axis=0))
    qw, qx, qy, qz = (unit[0], unit[1], unit[2], unit[3])
    return jnp.stack([1 - 2 * (qy * qy + qz * qz), 2 * (qx * qy - qw * qz), 2 * (qx * qz + qw * qy), 2 * (qx * qy + qw * qz), 1 - 2 * (qx * qx + qz * qz), 2 * (qy * qz - qw * qx), 2 * (qx * qz - qw * qy), 2 * (qy * qz + qw * qx), 1 - 2 * (qx * qx + qy * qy)])


def pair_signs(key):
    flips = jax.random.bernoulli(jax.random.fold_in(key, 77), 0.5, (CZ, H))
    return jnp.where(flips, 1.0, -1.0).astype(jnp.float32)


def draw_query_single(key, part):
    key = jax.random.fold_in(key, 11)
    base = jnp.clip(jax.random.normal(key, (QUERIES, D), jnp.float32), -5.0, 5.0)
    ramp = jnp.arange(D, dtype=jnp.float32) / D
    scale = 0.5 * 3.0 ** ramp
    return (base * scale[None, :]).astype(jnp.bfloat16)


def draw_query_rotation(key, part):
    key = jax.random.fold_in(key, 12)
    return rotation_table(key, QUERIES)


def draw_key_rotation(key, part):
    key = jax.random.fold_in(key, 13)
    return rotation_table(key, KEYS)


def draw_pair_weight(key, part):
    signs = pair_signs(key)
    key = jax.random.fold_in(key, 21)
    magnitude = jnp.abs(jnp.clip(jax.random.normal(key, (CZ, H), jnp.float32), -4.0, 4.0))
    return (signs * magnitude * CZ ** (-0.5)).astype(jnp.bfloat16)


def draw_pair_tile(key, part):
    key = jax.random.fold_in(key, 22)
    base = jnp.clip(jax.random.normal(key, (QUERIES, KEYS, CZ), jnp.float32), -5.0, 5.0)
    return base.astype(jnp.bfloat16)


def draw_out_weight(key, part):
    key = jax.random.fold_in(key, 31)
    base = jnp.clip(jax.random.normal(key, (OUT_FEAT, D), jnp.float32), -5.0, 5.0)
    ramp = jnp.arange(D, dtype=jnp.float32) / D
    scale = 0.6 * 3.0 ** ramp
    return (base * scale[None, :] * OUT_FEAT ** (-0.5)).astype(jnp.bfloat16)


def place_ends(drawn, stream_key, smallest, top_value):
    dims = drawn.shape
    spot = [jax.random.randint(jax.random.fold_in(stream_key, axis), (), 0, dims[axis]) for axis in range(len(dims))]
    drawn = drawn.at[tuple(spot)].set(smallest)
    longest = dims.index(max(dims))
    spot[longest] = (spot[longest] + 1) % dims[longest]
    return drawn.at[tuple(spot)].set(top_value)


def block_scale(stream_key, dims, pieces, smallest, top_value):
    level, own = 1.0, jax.random.fold_in(stream_key, 6)
    for dim, blocks in pieces:
        steps = jnp.exp(jax.random.uniform(jax.random.fold_in(own, dim), (blocks,), jnp.float32, smallest / len(pieces), top_value / len(pieces)))
        level = level * jnp.repeat(steps, dims[dim] // blocks).reshape([-1 if axis == dim else 1 for axis in range(len(dims))])
    return level


def length_profile(amount, total, bound, slope):
    loads = [(1 << 20) // math.isqrt(grade ** slope) + 1 for grade in range(2, amount + 1)]
    spare, given = total - bound - (amount - 1), [1] * (amount - 1)
    while spare > 0:
        movable = [i for i in range(amount - 1) if given[i] < bound]
        whole, remaining = sum([loads[i] for i in movable]), spare
        for i in movable:
            more = min(bound - given[i], max(1, remaining * loads[i] // whole), spare)
            given[i] = given[i] + more
            spare = spare - more
    return np.array([bound] + given)


def uneven_parts(own_key, count, total, limit, slope):
    if count == 2:
        one = jax.random.randint(own_key, (), max(1, total - limit), min(limit, total - 1) + 1)
        return jnp.stack([one, total - one])
    lengths = jnp.asarray(length_profile(count, total, limit, slope), jnp.int32)
    pairs = (count - 1) // 2
    source_of, sink = lengths[1:1 + 2 * pairs:2], lengths[2:2 + 2 * pairs:2]
    margin = jnp.minimum(source_of - 1, limit - sink)
    moved = jax.random.randint(jax.random.fold_in(own_key, 1), (pairs,), 0, 1 << 20) % (margin + 1)
    lengths = lengths.at[1:1 + 2 * pairs:2].set(source_of - moved).at[2:2 + 2 * pairs:2].set(sink + moved)
    return lengths[jax.random.permutation(jax.random.fold_in(own_key, 2), count)]


def noise(stream_key, dims, scale, limit, split=(), kind=jnp.bfloat16):
    result = scale * jax.random.normal(stream_key, dims, jnp.float32)
    if split:
        result = result * block_scale(stream_key, dims, split, -0.22, 0.18)
    return jnp.clip(result, -limit, limit).astype(kind)


def setup_inputs(seed: int = 0) -> dict:
    arg_keys = jax.random.split(jax.random.key(seed), 23)
    query_single = draw_query_single(jax.random.fold_in(arg_keys[22], 71), 0)
    query_rotation = draw_query_rotation(jax.random.fold_in(arg_keys[22], 71), 0)
    query_anchor = noise(arg_keys[2], (3, QUERIES), 1.0, 5.0, ((1, 8),), jnp.float32)
    query_chain = jnp.searchsorted(jnp.cumsum(uneven_parts(arg_keys[3], CHAINS, QUERIES, QUERIES // 8, 2)), jnp.arange(QUERIES), side="right").astype(jnp.int32)
    key_single = noise(arg_keys[4], (KEYS, D), 1.0, 5.0, ((0, 128),))
    key_rotation = draw_key_rotation(jax.random.fold_in(arg_keys[22], 71), 0)
    key_anchor = noise(arg_keys[6], (3, KEYS), 1.0, 5.0, ((1, 128),), jnp.float32)
    key_chain = jnp.searchsorted(jnp.cumsum(uneven_parts(arg_keys[7], CHAINS, KEYS, KEYS // 8, 2)), jnp.arange(KEYS), side="right").astype(jnp.int32)
    key_mask = place_ends((jax.random.randint(arg_keys[8], (KEYS,), 0, 8) < 7).astype(jnp.int32), jax.random.fold_in(arg_keys[8], 1), 0, 1)
    pair_tile = draw_pair_tile(jax.random.fold_in(arg_keys[22], 71), 0)
    query_weight = noise(arg_keys[10], (D, H * C), D ** -0.5, 0.3125)
    query_point_weight = noise(arg_keys[11], (D, 3 * H * PQ), D ** -0.5, 0.3125)
    key_weight = noise(arg_keys[12], (D, H * C), D ** -0.5, 0.3125)
    value_weight = noise(arg_keys[13], (D, H * C), D ** -0.5, 0.3125)
    key_point_weight = noise(arg_keys[14], (D, 3 * H * PQ), D ** -0.5, 0.3125)
    value_point_weight = noise(arg_keys[15], (D, 3 * H * PV), D ** -0.5, 0.3125)
    pair_weight = draw_pair_weight(jax.random.fold_in(arg_keys[22], 71), 0)
    head_gamma = jnp.clip(jnp.exp(jax.random.uniform(arg_keys[17], (H,), jnp.float32, math.log(0.05), math.log(1.0))), 0.05, 1.0)
    chain_gap = jnp.clip(jax.random.uniform(arg_keys[18], (H,), jnp.float32, -3.0, 3.0), -3.0, 3.0)
    out_weight = draw_out_weight(jax.random.fold_in(arg_keys[22], 71), 0)
    norm_gain = jnp.clip(1.0 + 0.18 * jax.random.normal(arg_keys[20], (D,), jnp.float32), 0.1, 1.9)
    norm_shift = noise(arg_keys[21], (D,), 0.5, 3.0, ((0, 16),), jnp.float32)
    return {"query_single": query_single, "query_rotation": query_rotation, "query_anchor": query_anchor, "query_chain": query_chain, "key_single": key_single, "key_rotation": key_rotation, "key_anchor": key_anchor, "key_chain": key_chain, "key_mask": key_mask, "pair_tile": pair_tile, "query_weight": query_weight, "query_point_weight": query_point_weight, "key_weight": key_weight, "value_weight": value_weight, "key_point_weight": key_point_weight, "value_point_weight": value_point_weight, "pair_weight": pair_weight, "head_gamma": head_gamma, "chain_gap": chain_gap, "out_weight": out_weight, "norm_gain": norm_gain, "norm_shift": norm_shift}


LOGIT_SCALE = (1.0 / 3.0) ** 0.5
NORM_EPS = 1e-05
MASKED = -1000000000.0
PRECISE = lax.Precision.HIGHEST

def wide_dot(left, right):
    return jnp.dot(left.astype(jnp.float32), right.astype(jnp.float32), precision=PRECISE, preferred_element_type=jnp.float32)

def rotate(rotation, local_points, translation):
    moved = []
    for component in range(3):
        moved.append(rotation[3 * component] * local_points[0] + rotation[3 * component + 1] * local_points[1] + rotation[3 * component + 2] * local_points[2] + translation[component])
    return jnp.stack(moved)

def key_package(residues, rotation, translation, key_weight, value_weight, key_point_weight, value_point_weight):
    residue_count = residues.shape[0]
    weights = jnp.concatenate([key_weight, value_weight, key_point_weight, value_point_weight], axis=1)
    projected = wide_dot(residues, weights).T
    first_cut = 2 * H * C
    second_cut = first_cut + 3 * H * PQ
    key_points = rotate(rotation, projected[first_cut:second_cut].reshape(3, H * PQ, residue_count), translation)
    value_points = rotate(rotation, projected[second_cut:].reshape(3, H * PV, residue_count), translation)
    return jnp.concatenate([projected[:first_cut], key_points.reshape(3 * H * PQ, residue_count), value_points.reshape(3 * H * PV, residue_count)], axis=0).astype(jnp.bfloat16)

def block_partials(queries, query_points, query_chain, package, key_chain, key_mask, pair, pair_weight, head_gamma, chain_gap):
    key_count = package.shape[1]
    query_count = queries.shape[2]
    first_cut = 2 * H * C
    second_cut = first_cut + 3 * H * PQ
    keys_block = package[:H * C].astype(jnp.float32).reshape(H, C, key_count)
    values_block = package[H * C:first_cut].astype(jnp.float32).reshape(H, C, key_count)
    key_points = package[first_cut:second_cut].astype(jnp.float32).reshape(3, H, PQ, key_count)
    value_points = package[second_cut:].astype(jnp.float32).reshape(3, H, PV, key_count)
    pair_wide = pair.astype(jnp.float32)
    affinity = jnp.einsum('hcq,hck->hqk', queries.astype(jnp.float32), keys_block, precision=PRECISE)
    pair_bias = jnp.einsum('qkc,ch->hqk', pair_wide, pair_weight.astype(jnp.float32), precision=PRECISE)
    inner_products = jnp.einsum('ahpq,ahpk->hqk', query_points, key_points, precision=PRECISE)
    query_norms = lax.optimization_barrier(jnp.sum(query_points * query_points, axis=(0, 2)))
    key_norms = lax.optimization_barrier(jnp.sum(key_points * key_points, axis=(0, 2)))
    distances = query_norms[:, :, None] + key_norms[:, None, :] - 2.0 * inner_products
    chain_apart = (query_chain[:, None] != key_chain[None, :]).astype(jnp.float32)
    point_scale = head_gamma * (2.0 / (9.0 * PQ)) ** 0.5 * 0.5
    logits = LOGIT_SCALE * (affinity * C ** (-0.5) + pair_bias + chain_gap[:, None, None] * chain_apart[None] - point_scale[:, None, None] * distances)
    logits = jnp.where(key_mask[None, None, :] > 0, logits, MASKED)
    maximum = lax.optimization_barrier(jnp.max(logits, axis=-1))
    attention = jnp.exp(logits - maximum[:, :, None]).astype(jnp.bfloat16).astype(jnp.float32)
    weight_sum = lax.optimization_barrier(jnp.sum(attention, axis=-1))
    value_part = jnp.einsum('hqk,hck->hcq', attention, values_block, precision=PRECISE)
    point_part = jnp.einsum('hqk,ahpk->hapq', attention, value_points, precision=PRECISE).reshape(H, 3 * PV, query_count)
    pair_part = jnp.einsum('hqk,qkc->hcq', attention, pair_wide, precision=PRECISE)
    return (maximum, weight_sum, jnp.concatenate([value_part, point_part, pair_part], axis=1))

def finish(weight_sum, numerators, rotation, translation):
    averaged = numerators / weight_sum[:, None, :]
    global_points = averaged[:, C:C + 3 * PV].reshape(H, 3, PV, -1)
    shifted = global_points - translation[None, :, None, :]
    local_list = []
    for component in range(3):
        local_list.append(rotation[component] * shifted[:, 0] + rotation[3 + component] * shifted[:, 1] + rotation[6 + component] * shifted[:, 2])
    local_points = jnp.stack(local_list, axis=1).reshape(H, 3 * PV, -1)
    joined = jnp.concatenate([averaged[:, :C], local_points, averaged[:, C + 3 * PV:]], axis=1)
    return joined.reshape(H * FEAT, -1).astype(jnp.bfloat16)

def reference(query_single, query_rotation, query_anchor, query_chain, key_single, key_rotation, key_anchor, key_chain, key_mask, pair_tile, query_weight, query_point_weight, key_weight, value_weight, key_point_weight, value_point_weight, pair_weight, head_gamma, chain_gap, out_weight, norm_gain, norm_shift):
    package = key_package(key_single, key_rotation, key_anchor, key_weight, value_weight, key_point_weight, value_point_weight)
    projected = wide_dot(query_single, jnp.concatenate([query_weight, query_point_weight], axis=1)).T
    queries = projected[:H * C].astype(jnp.bfloat16).reshape(H, C, QUERIES)
    query_points = rotate(query_rotation, projected[H * C:].reshape(3, H * PQ, QUERIES), query_anchor).reshape(3, H, PQ, QUERIES)

    def one_query_block(query_block):
        query_start = (query_block * Q_DEV).astype(jnp.int32)
        block_queries = lax.dynamic_slice_in_dim(queries, query_start, Q_DEV, 2)
        block_points = lax.dynamic_slice_in_dim(query_points, query_start, Q_DEV, 3)
        block_chain = lax.dynamic_slice_in_dim(query_chain, query_start, Q_DEV, 0)
        block_rotation = lax.dynamic_slice_in_dim(query_rotation, query_start, Q_DEV, 1)
        block_anchor = lax.dynamic_slice_in_dim(query_anchor, query_start, Q_DEV, 1)

        def one_key_block(key_block):
            key_start = (key_block * K_DEV).astype(jnp.int32)
            block_package = lax.dynamic_slice_in_dim(package, key_start, K_DEV, 1)
            block_keys_chain = lax.dynamic_slice_in_dim(key_chain, key_start, K_DEV, 0)
            block_mask = lax.dynamic_slice_in_dim(key_mask, key_start, K_DEV, 0)
            pair = lax.dynamic_slice(pair_tile, (query_start, key_start, jnp.int32(0)), (Q_DEV, K_DEV, CZ))
            return block_partials(block_queries, block_points, block_chain, block_package, block_keys_chain, block_mask, pair, pair_weight, head_gamma, chain_gap)
        maxima, sums, numerators = lax.map(one_key_block, jnp.arange(KEYS // K_DEV, dtype=jnp.int32))
        highest = lax.optimization_barrier(jnp.max(maxima, axis=0))
        factor = jnp.exp(maxima - highest[None])
        weight_sum = lax.optimization_barrier(jnp.sum(sums * factor, axis=0))
        combined = lax.optimization_barrier(jnp.sum(numerators * factor[:, :, None, :], axis=0))
        return finish(weight_sum, combined, block_rotation, block_anchor)
    features = lax.map(one_query_block, jnp.arange(QUERIES // Q_DEV, dtype=jnp.int32))
    features = jnp.transpose(features, (1, 0, 2)).reshape(H * FEAT, QUERIES)
    mixed = query_single.astype(jnp.float32) + wide_dot(features.T, out_weight)
    average = lax.optimization_barrier(jnp.mean(mixed, axis=1, keepdims=True))
    centred = mixed - average
    variance = lax.optimization_barrier(jnp.mean(centred * centred, axis=1, keepdims=True))
    return (centred * lax.rsqrt(variance + NORM_EPS) * norm_gain + norm_shift).astype(jnp.bfloat16)
```

```python
import jax
import jax.numpy as jnp
import numpy as np
from jax import lax
from jax.experimental import pallas as pl
from jax.experimental.pallas import tpu as pltpu
from jax.sharding import PartitionSpec as P

D = 384
H = 12
C = 16
PQ = 4
PV = 8
CZ = 128
FEAT = 168
QB = 8
RB = QB * H

LOGIT_SCALE = (1.0 / 3.0) ** 0.5
POINT_SCALE = (2.0 / (9.0 * PQ)) ** 0.5 * 0.5
NORM_EPS = 1e-05
MASKED = -1000000000.0
PRECISE = lax.Precision.HIGHEST
F32 = jnp.float32
BF16 = jnp.bfloat16

CHAIN_AT = H * C
POINTS_AT = CHAIN_AT + 3 * 16
NORMS_AT = POINTS_AT + 3 * 3 * H * PQ
DEPTH = NORMS_AT + 6 * 16
SUM_AT = H * C + 3 * H * PV
WIDE = 512
CHUNK = RB + 48


def head_masks():
    head = (np.arange(RB) % H)[:, None]
    k = np.arange(DEPTH)[None, :]
    of_k = np.where(
        k < CHAIN_AT,
        k // C,
        np.where(
            k < POINTS_AT,
            -1,
            np.where(k < NORMS_AT, ((k - POINTS_AT) % (H * PQ)) // PQ, (k - NORMS_AT) % 16),
        ),
    )
    f = np.arange(WIDE)[None, :]
    of_f = np.where(
        f < H * C,
        f // C,
        np.where(f < SUM_AT, ((f - H * C) % (H * PV)) // PV, f - SUM_AT),
    )
    lane = np.arange(128)[None, :]
    spread = (np.arange(128)[:, None] == of_f) & (f < SUM_AT)
    return (
        (head == of_k).astype(np.float32),
        (head == of_f).astype(np.float32),
        (head == lane).astype(np.float32),
        spread.astype(np.float32),
    )


def split(x):
    first = x.astype(BF16)
    rest = x - first.astype(F32)
    second = rest.astype(BF16)
    third = (rest - second.astype(F32)).astype(BF16)
    return first, second, third


def dot(a, b, ca=1, cb=0, precision=None):
    return lax.dot_general(
        a, b, (((ca,), (cb,)), ((), ())), precision=precision, preferred_element_type=F32
    )


def iota(shape, axis):
    return lax.broadcasted_iota(jnp.int32, shape, axis)


def row_of(rows, first):
    gap = iota((rows, 128), 0) - H * (iota((rows, 128), 1) - first)
    return jnp.where((gap >= 0) & (gap < H), 1.0, 0.0).astype(BF16)


def pack_kernel(cols, rows, qs, ks, krot, kanc, ow, q_out, k_out, w_out):
    turned = qs[...].astype(F32).T.astype(BF16)
    for c in range(cols):
        q_out[c] = turned
    frames = jnp.concatenate([krot[...], kanc[...], jnp.zeros((4, krot.shape[1]), F32)], axis=0)
    parts = jnp.concatenate([p.astype(F32) for p in split(frames)], axis=0)
    frames = jnp.concatenate([parts, jnp.zeros((80, krot.shape[1]), F32)], axis=0).T.astype(BF16)
    for r in range(rows):
        k_out[r, :, :D] = ks[...]
        k_out[r, :, D:] = frames
    w = ow[...].astype(F32)
    pieces = [w[h * FEAT + 40 : (h + 1) * FEAT] for h in range(H)]
    pieces += [w[h * FEAT : h * FEAT + C] for h in range(H)]
    for a in range(3):
        start = C + a * PV
        pieces += [w[h * FEAT + start : h * FEAT + start + PV] for h in range(H)]
    w = jnp.concatenate(pieces, axis=0).astype(BF16)
    width = w.shape[1]
    eye = jnp.where(iota((width, width), 0) == iota((width, width), 1), 1.0, 0.0).astype(BF16)
    w_out[...] = dot(eye, w, 1, 1).astype(BF16)


def bias_kernel(pair, pw, out):
    gap = iota((2 * H, H), 0) - iota((2 * H, H), 1)
    pick = jnp.where((gap == 0) | (gap == H), 1.0, 0.0).astype(BF16)
    turned = dot(pick, pw[...], 1, 1)
    row = iota((2 * H, CZ), 0)
    weights = jnp.concatenate(
        [jnp.where(row < H, turned, 0.0), jnp.where(row < H, 0.0, turned)], axis=1
    ).astype(BF16)
    for p in range(QB // 2):
        both = jnp.concatenate([pair[2 * p], pair[2 * p + 1]], axis=1)
        out[2 * H * p : 2 * H * (p + 1)] = dot(weights, both, 1, 1)


def rotated(rot, anc, local):
    size = local.shape[0] // 3
    part = [local[size * b : size * (b + 1)] for b in range(3)]
    return [
        rot[3 * a : 3 * a + 1] * part[0]
        + rot[3 * a + 1 : 3 * a + 2] * part[1]
        + rot[3 * a + 2 : 3 * a + 3] * part[2]
        + anc[a : a + 1]
        for a in range(3)
    ]


def attend_kernel(
    blocks,
    qall,
    qrot,
    qanc,
    qchain,
    kall,
    kchain,
    kmask,
    qw,
    qpw,
    kw,
    vw,
    kpw,
    vpw,
    gamma,
    gap,
    mask_k,
    mask_f,
    mask_h,
    bias,
    pair_hbm,
    out,
    pair,
    left,
    logits,
    attn,
    extra,
    sems,
):
    def fetch(b):
        return pltpu.make_async_copy(
            pair_hbm.at[pl.ds(QB * b, QB)], pair.at[pl.ds(QB * b, QB)], sems.at[b]
        )

    for b in range(blocks):
        fetch(b).start()

    scale = gamma[...] * POINT_SCALE
    by_point = jnp.where((iota((H * PQ, H), 0) >> 2) == iota((H * PQ, H), 1), scale, 0.0)
    by_point = jnp.sum(by_point, axis=1, keepdims=True)
    by_head = jnp.where(iota((16, H), 0) == iota((16, H), 1), scale, 0.0)
    by_head = jnp.sum(by_head, axis=1, keepdims=True)
    heads = jnp.where(iota((16, H * PQ), 0) == (iota((16, H * PQ), 1) >> 2), 1.0, 0.0)

    def norms(points):
        squares = points[0] * points[0] + points[1] * points[1] + points[2] * points[2]
        return split(-by_head * dot(heads, squares, precision=PRECISE))

    q = dot(qw[...], qall[...], 0, 0).astype(BF16).astype(F32) * C ** (-0.5)
    points = rotated(qrot[...], qanc[...], dot(qpw[...], qall[...], 0, 0))
    first, second, third = split(jnp.concatenate([2.0 * by_point * p for p in points], axis=0))
    count = qall.shape[1]
    chain = jnp.where(iota((16, count), 0) == qchain[...], 1.0, 0.0).astype(BF16)
    ones = jnp.ones((16, count), BF16)
    table = jnp.concatenate(
        [q.astype(BF16), chain, chain, chain, first, second, third, *norms(points), ones, ones, ones],
        axis=0,
    )

    rows = kall[:, :D]
    keys = kall.shape[0]
    eye = jnp.where(iota((128, 128), 0) == iota((128, 128), 1), 1.0, 0.0).astype(BF16)
    frames = dot(eye, kall[:, D:], 1, 1)
    frames = (frames[0:16] + frames[16:32]) + frames[32:48]
    krot, kanc = frames[0:9], frames[9:12]

    def project(weight):
        return dot(weight[...], rows, 0, 1)

    kpoints = [p.astype(BF16) for p in rotated(krot, kanc, project(kpw))]
    vpoints = [p.astype(BF16) for p in rotated(krot, kanc, project(vpw))]
    apart = jnp.where(iota((16, keys), 0) != kchain[...], 1.0, 0.0).astype(BF16)
    kones = jnp.ones((16, keys), BF16)
    right = jnp.concatenate(
        [
            project(kw).astype(BF16),
            apart,
            apart,
            apart,
            *kpoints,
            *kpoints,
            *kpoints,
            kones,
            kones,
            kones,
            *norms([p.astype(F32) for p in kpoints]),
        ],
        axis=0,
    )
    values = jnp.concatenate(
        [project(vw).astype(BF16), *vpoints, kones, jnp.zeros((16, keys), BF16)], axis=0
    )

    head_lane = mask_h[...]
    own_gap = jnp.sum(head_lane[:, :H] * gap[...], axis=1, keepdims=True)
    lane = iota((RB, DEPTH), 1)
    by_column = mask_k[...]
    for t, part in enumerate(split(own_gap)):
        inside = (lane >= CHAIN_AT + 16 * t) & (lane < CHAIN_AT + 16 * (t + 1))
        by_column = jnp.where(inside, part.astype(F32), by_column)
    for b in range(blocks):
        left[RB * b : RB * (b + 1)] = (dot(row_of(RB, QB * b), table, 1, 1) * by_column).astype(BF16)
    tall = 4 * RB
    for g in range(blocks // 4):
        logits[tall * g : tall * (g + 1)] = dot(left[tall * g : tall * (g + 1)], right)

    real = kmask[...] > 0
    lanes = [head_lane] + [pltpu.roll(head_lane, 16 * t, 1) for t in range(1, 4)]
    for b in range(blocks):
        at = slice(RB * b, RB * (b + 1))
        x = jnp.where(real, LOGIT_SCALE * (logits[at] + bias[at]), MASKED)
        top = jnp.max(x, axis=1, keepdims=True)
        e = jnp.exp(x - top)
        attn[at] = e.astype(BF16)
        tops = [p.astype(F32) for p in split(top)]
        extra[at] = tops[0] * lanes[0] + tops[1] * lanes[1] + tops[2] * lanes[2]
        fetch(b).wait()
        upper = iota((2 * H, CZ), 0) < H
        for p in range(QB // 2):
            i = QB * b + 2 * p
            both = jnp.concatenate([pair[i], pair[i + 1]], axis=1)
            z = dot(e[2 * H * p : 2 * H * (p + 1)].astype(BF16), both)
            z = jnp.where(upper, z[:, :CZ], z[:, CZ:])
            logits[RB * b + 2 * H * p : RB * b + 2 * H * (p + 1), :CZ] = z
        out[b, :RB] = logits[at, :CZ].astype(BF16)

    by_lane = mask_f[...]
    own = iota((QB, RB), 1) - H * iota((QB, RB), 0)
    own = jnp.where((own >= 0) & (own < H), 1.0, 0.0).astype(BF16)
    for g in range(blocks // 4):
        wide = dot(attn[tall * g : tall * (g + 1)], values, 1, 1)
        for s in range(4):
            b = 4 * g + s
            mine = wide[RB * s : RB * (s + 1)] * by_lane
            rounded = mine.astype(BF16)
            last = mine[:, 384:] - rounded[:, 384:].astype(F32)
            rest = extra[RB * b : RB * (b + 1)] + pltpu.roll(last, 80, 1) * lanes[3]
            packed = dot(own, rounded)
            tail = dot(own, rest.astype(BF16))
            out[b, RB:] = jnp.concatenate(
                [packed[:, 128 * t : 128 * (t + 1)] for t in range(4)]
                + [tail, jnp.zeros((8, 128), F32)],
                axis=0,
            ).astype(BF16)


def finish_kernel(cols, got, qall, qrot, qanc, weights, mask_h, spread, out, rows):
    tail = got[:, RB:, :].astype(F32)
    count = cols * QB

    def tile(t):
        return tail[:, QB * t : QB * (t + 1)].reshape(count, 128)

    marks = tile(4)
    top = (marks + pltpu.roll(marks, 112, 1)) + pltpu.roll(marks, 96, 1)
    sums = pltpu.roll(tile(3), 32, 1) + pltpu.roll(marks, 80, 1)
    top = top.reshape(cols, QB, 128)
    factor = jnp.exp(top - jnp.max(top, axis=0, keepdims=True))
    total = jnp.sum(sums.reshape(cols, QB, 128) * factor, axis=0, keepdims=True)
    head = iota((cols, QB, 128), 2) < H
    factor = jnp.where(head, factor / total, 0.0).reshape(count, 128)
    high, low, _ = split(factor)
    wide = dot(high, spread[...]) + dot(low, spread[...])
    averaged = [
        jnp.sum((tile(t) * wide[:, 128 * t : 128 * (t + 1)]).reshape(cols, QB, 128), axis=0)
        for t in range(4)
    ]
    averaged = jnp.concatenate(averaged, axis=1)

    z = jnp.zeros((RB, CZ), F32)
    for c in range(cols):
        pick = row_of(RB, QB * c)
        mine = (dot(pick, high) + dot(pick, low)) * mask_h[...]
        z = z + got[c, :RB].astype(F32) * jnp.sum(mine, axis=1, keepdims=True)
    rows[...] = z

    me = lax.axis_index("col")
    own = iota((QB, 128), 1) == QB * me + iota((QB, 128), 0)

    def mine(ref, k):
        return jnp.sum(jnp.where(own, ref[k : k + 1], 0.0), axis=1, keepdims=True)

    cut = H * C
    step = H * PV
    shifted = [averaged[:, cut + step * b : cut + step * (b + 1)] - mine(qanc, b) for b in range(3)]
    local = [
        mine(qrot, a) * shifted[0] + mine(qrot, 3 + a) * shifted[1] + mine(qrot, 6 + a) * shifted[2]
        for a in range(3)
    ]
    features = [rows[pl.ds(h, QB, stride=H), :] for h in range(H)] + [averaged[:, :cut]] + local
    features = jnp.concatenate(features, axis=1).astype(BF16)
    mixed = dot(jnp.where(own, 1.0, 0.0).astype(BF16), qall[...], 1, 1)
    mixed = mixed + dot(features, weights[...], 1, 1)
    centred = mixed - jnp.sum(mixed, axis=1, keepdims=True) * (1.0 / D)
    variance = jnp.sum(centred * centred, axis=1, keepdims=True) * (1.0 / D)
    normal = centred * lax.rsqrt(variance + NORM_EPS)
    width = D // cols
    for c in range(cols):
        out[c] = normal[:, width * c : width * (c + 1)]


def call(kernel, out_shape, scratch=(), **params):
    return pl.pallas_call(
        kernel,
        out_shape=out_shape,
        scratch_shapes=scratch,
        compiler_params=pltpu.CompilerParams(vmem_limit_bytes=48 << 20, **params),
    )


def shape(dims, dtype):
    return jax.ShapeDtypeStruct(dims, dtype)


def on_device(
    query_single,
    query_rotation,
    query_anchor,
    query_chain,
    key_single,
    key_rotation,
    key_anchor,
    key_chain,
    key_mask,
    pair_tile,
    query_weight,
    query_point_weight,
    key_weight,
    value_weight,
    key_point_weight,
    value_point_weight,
    pair_weight,
    head_gamma,
    chain_gap,
    out_weight,
    norm_gain,
    norm_shift,
):
    rows, cols = lax.axis_size("row"), lax.axis_size("col")
    queries, width = query_single.shape
    own_keys = key_single.shape[0]
    keys = rows * own_keys
    blocks = queries // QB
    mask_k, mask_f, mask_h, spread = (jnp.asarray(m) for m in head_masks())

    def send(x, axis):
        return lax.all_to_all(x, axis, 0, 0)

    q_pack, k_pack, w_pack = call(
        lambda *refs: pack_kernel(cols, rows, *refs),
        (
            shape((cols, width, queries), BF16),
            shape((rows, own_keys, 512), BF16),
            shape((width, H * FEAT), BF16),
        ),
    )(query_single, key_single, key_rotation, key_anchor, out_weight)
    qall = send(q_pack, "col").reshape(D, queries)
    kall = send(k_pack, "row").reshape(keys, 512)
    weights = lax.all_gather(w_pack, "col", axis=0, tiled=True)

    bias = pl.pallas_call(
        bias_kernel,
        grid=(blocks,),
        in_specs=[
            pl.BlockSpec((QB, keys, CZ), lambda b: (b, 0, 0)),
            pl.BlockSpec((CZ, H), lambda b: (0, 0)),
        ],
        out_specs=pl.BlockSpec((RB, keys), lambda b: (b, 0)),
        out_shape=shape((blocks * RB, keys), F32),
        compiler_params=pltpu.CompilerParams(vmem_limit_bytes=32 << 20),
        cost_estimate=pl.CostEstimate(
            flops=2 * queries * keys * CZ * 128,
            bytes_accessed=queries * keys * CZ * 2,
            transcendentals=0,
        ),
    )(pair_tile, pair_weight)

    whole = pl.BlockSpec(memory_space=pltpu.VMEM)
    parts = pl.pallas_call(
        lambda *refs: attend_kernel(blocks, *refs),
        in_specs=[whole] * 19 + [pl.BlockSpec(memory_space=pl.ANY)],
        out_specs=whole,
        out_shape=shape((blocks, CHUNK, 128), BF16),
        scratch_shapes=[
            pltpu.VMEM((queries, keys, CZ), BF16),
            pltpu.VMEM((blocks * RB, DEPTH), BF16),
            pltpu.VMEM((blocks * RB, keys), F32),
            pltpu.VMEM((blocks * RB, keys), BF16),
            pltpu.VMEM((blocks * RB, 128), F32),
            pltpu.SemaphoreType.DMA((blocks,)),
        ],
        compiler_params=pltpu.CompilerParams(vmem_limit_bytes=48 << 20),
    )(
        qall,
        query_rotation,
        query_anchor,
        query_chain.reshape(1, -1),
        kall,
        key_chain.reshape(1, -1),
        key_mask.reshape(1, -1),
        query_weight,
        query_point_weight,
        key_weight,
        value_weight,
        key_point_weight,
        value_point_weight,
        head_gamma.reshape(1, -1),
        chain_gap.reshape(1, -1),
        mask_k,
        mask_f,
        mask_h,
        bias,
        pair_tile,
    )
    got = send(parts, "col")
    normal = call(
        lambda *refs: finish_kernel(cols, *refs),
        shape((cols, QB, width), F32),
        [pltpu.VMEM((RB, CZ), F32)],
    )(got, qall, query_rotation, query_anchor, weights, mask_h, spread.astype(BF16))
    normal = send(normal, "col").reshape(queries, width)
    return (normal * norm_gain + norm_shift).astype(BF16)


def solution(mesh):
    placed = (
        P("row", "col"),
        P(None, "row"),
        P(None, "row"),
        P("row"),
        P(("col", "row"), None),
        P(None, ("col", "row")),
        P(None, ("col", "row")),
        P("col"),
        P("col"),
        P("row", "col", None),
        P(),
        P(),
        P(),
        P(),
        P(),
        P(),
        P(),
        P(),
        P(),
        P(None, "col"),
        P("col"),
        P("col"),
    )
    return jax.shard_map(
        on_device, mesh=mesh, in_specs=placed, out_specs=P("row", "col"), check_vma=False
    )
```

```python
import jax
import jax.numpy as jnp
from jax import lax
from jax.experimental import pallas as pl
from jax.experimental.pallas import tpu as pltpu
from jax.sharding import PartitionSpec as P

D = 384
H = 12
C = 16
PQ = 4
PV = 8
CZ = 128
FEAT = 168
QB = 8
RB = QB * H

LOGIT_SCALE = (1.0 / 3.0) ** 0.5
POINT_SCALE = (2.0 / (9.0 * PQ)) ** 0.5 * 0.5
NORM_EPS = 1e-05
MASKED = -1000000000.0
PRECISE = lax.Precision.HIGHEST
F32 = jnp.float32
BF16 = jnp.bfloat16

CHAIN_AT = H * C
POINTS_AT = CHAIN_AT + 3 * 16
NORMS_AT = POINTS_AT + 3 * 3 * H * PQ
DEPTH = NORMS_AT + 6 * 16
SUM_AT = H * C + 3 * H * PV
WIDE = 512
VMEM_BYTES = 63_400_000
SMALL = 11
KEY_SMALL = 12
AHEAD = 8
TALL = 8
HALF = 1024
CHUNK = RB + 48


def split(x):
    first = x.astype(BF16)
    rest = x - first.astype(F32)
    second = rest.astype(BF16)
    third = (rest - second.astype(F32)).astype(BF16)
    return first, second, third


def dot(a, b, ca=1, cb=0, precision=None):
    return lax.dot_general(
        a, b, (((ca,), (cb,)), ((), ())), precision=precision, preferred_element_type=F32
    )


def iota(shape, axis):
    return lax.broadcasted_iota(jnp.int32, shape, axis)


def head_row(shape_):
    row = iota(shape_, 0)
    return row - H * ((row * 43) >> 9)


def column_heads():
    k = iota((RB, DEPTH), 1)
    point = k - POINTS_AT
    for _ in range(8):
        point = jnp.where(point >= H * PQ, point - H * PQ, point)
    of_chain = jnp.where(k < POINTS_AT, -1, point >> 2)
    return jnp.where(k < CHAIN_AT, k >> 4, jnp.where(k < NORMS_AT, of_chain, (k - NORMS_AT) & 15))


def value_heads(shape_):
    f = iota(shape_, 1)
    point = f - H * C
    for _ in range(2):
        point = jnp.where(point >= H * PV, point - H * PV, point)
    return jnp.where(f < H * C, f >> 4, jnp.where(f < SUM_AT, point >> 3, f - SUM_AT))


def row_of(rows, first):
    gap = iota((rows, 128), 0) - H * (iota((rows, 128), 1) - first)
    return jnp.where((gap >= 0) & (gap < H), 1.0, 0.0).astype(BF16)


def fetch_all(pairs, sems):
    copies = [pltpu.make_async_copy(src, dst, sems.at[k]) for k, (src, dst) in enumerate(pairs)]
    for c in copies:
        c.start()
    return copies


def pack_kernel(qs_in, ks_in, krot_in, kanc_in, q_out, k_out, qs, frames, sems):
    own = ks_in.shape[0]
    copies = fetch_all(
        [
            (krot_in, frames.at[pl.ds(0, 9)]),
            (kanc_in, frames.at[pl.ds(16, 3)]),
            (qs_in, qs),
            (ks_in, k_out.at[:, pl.ds(0, D)]),
        ],
        sems,
    )
    copies[0].wait()
    copies[1].wait()
    row = iota((24, own), 0)
    both = jnp.where((row < 9) | ((row >= 16) & (row < 19)), frames[...], 0.0)
    parts = [p.astype(F32) for p in split(both)]
    parts = jnp.concatenate(parts + [jnp.zeros((56, own), F32)], axis=0)
    k_out[:, D:] = parts.T.astype(BF16)
    copies[2].wait()
    for c in range(q_out.shape[0]):
        q_out[c] = qs[...]
    copies[3].wait()


def rotated(rot, anc, local):
    size = local.shape[0] // 3
    part = [local[size * b : size * (b + 1)] for b in range(3)]
    return [
        rot[3 * a : 3 * a + 1] * part[0]
        + rot[3 * a + 1 : 3 * a + 2] * part[1]
        + rot[3 * a + 2 : 3 * a + 3] * part[2]
        + anc[a : a + 1]
        for a in range(3)
    ]


def lane_sums(table, wanted):
    return jnp.sum(jnp.where(wanted, table, 0.0), axis=1, keepdims=True)


def norms_of(points, scale):
    heads = jnp.where(iota((16, H * PQ), 0) == (iota((16, H * PQ), 1) >> 2), 1.0, 0.0)
    by_head = lane_sums(scale, iota((16, H), 0) == iota((16, H), 1))
    squares = points[0] * points[0] + points[1] * points[1] + points[2] * points[2]
    return split(-by_head * dot(heads, squares, precision=PRECISE))


def key_kernel(*refs):
    small_hbm, (w_out, key_out, column_out) = refs[:KEY_SMALL], refs[KEY_SMALL : KEY_SMALL + 3]
    small = refs[KEY_SMALL + 3 : 2 * KEY_SMALL + 3]
    w_pad, key_side, columns, kall, sems, more = refs[2 * KEY_SMALL + 3 :]
    copies = fetch_all(list(zip(small_hbm, small)), sems)
    for c in copies:
        c.wait()
    w, k0, k1, k2, k3, kchain, kw, vw, kpw, vpw, gamma, gap = small
    half = w_pad.shape[1] // 2
    width = w.shape[1]
    w_pad[:, :width] = w[...]
    w_pad[:, width:] = jnp.zeros((w.shape[0], 2 * half - width), BF16)
    core = lax.rem(lax.axis_index("row"), 2)
    mine = pl.ds(pl.multiple_of(core * half, half), half)
    cols = w_out.shape[0]
    stores = fetch_all([(w_pad.at[:, mine], w_out.at[c]) for c in range(cols)], more)

    chips = 4
    here = lax.axis_index("row") // 2
    size = k0.shape[0]
    for d, block in enumerate((k0, k1, k2, k3)):
        at = pl.multiple_of(lax.rem(here + chips - d, chips) * size, size)
        kall[pl.ds(at, size), :] = block[...]

    rows = kall[:, :D]
    keys = kall.shape[0]
    eye = jnp.where(iota((128, 128), 0) == iota((128, 128), 1), 1.0, 0.0).astype(BF16)
    frames = dot(eye, kall[:, D:], 1, 1)
    frames = (frames[0:24] + frames[24:48]) + frames[48:72]
    krot, kanc = frames[0:9], frames[16:19]

    def project(weight):
        return dot(weight[...], rows, 1, 1)

    kpoints = [p.astype(BF16) for p in rotated(krot, kanc, project(kpw))]
    vpoints = [p.astype(BF16) for p in rotated(krot, kanc, project(vpw))]
    apart = jnp.where(iota((16, keys), 0) != kchain[...], 1.0, 0.0).astype(BF16)
    ones = jnp.ones((16, keys), BF16)
    norms = norms_of([p.astype(F32) for p in kpoints], gamma[...] * POINT_SCALE)
    pieces = [project(kw).astype(BF16), apart, apart, apart, *kpoints, *kpoints, *kpoints]
    pieces += [ones, ones, ones, *norms]
    pieces += [project(vw).astype(BF16), *vpoints, ones, jnp.zeros((16, keys), BF16)]
    at = 0
    for piece in pieces:
        key_side[at : at + piece.shape[0]] = piece
        at += piece.shape[0]

    own_gap = lane_sums(gap[...], head_row((RB, H)) == iota((RB, H), 1))
    lane = iota((RB, DEPTH), 1)
    by_column = jnp.where(head_row((RB, DEPTH)) == column_heads(), 1.0, 0.0)
    for t, part in enumerate(split(own_gap)):
        inside = (lane >= CHAIN_AT + 16 * t) & (lane < CHAIN_AT + 16 * (t + 1))
        by_column = jnp.where(inside, part.astype(F32), by_column)
    columns[:, :DEPTH] = by_column
    columns[:, DEPTH:] = jnp.where(head_row((RB, WIDE)) == value_heads((RB, WIDE)), 1.0, 0.0)
    stores.append(pltpu.make_async_copy(key_side, key_out, more.at[cols]))
    stores.append(pltpu.make_async_copy(columns, column_out, more.at[cols + 1]))
    stores[cols].start()
    stores[cols + 1].start()

    for c in stores:
        c.wait()


def attend_kernel(pair_hbm, *refs):
    small_hbm, (out, aux), small = refs[:SMALL], refs[SMALL : SMALL + 2], refs[SMALL + 2 : 2 * SMALL + 2]
    pair, left, logits, attn, extra, pair_sems, sems = refs[2 * SMALL + 2 :]
    qall, qrot, qanc, qchain, qw, qpw, gamma, kmask, pw, columns, key_side = small
    blocks = pair.shape[0] // QB
    copies = fetch_all(list(zip(small_hbm, small)), sems)

    def fetch(b):
        at = pl.ds(QB * b, QB)
        return pltpu.make_async_copy(pair_hbm.at[at], pair.at[at], pair_sems.at[b])

    def start(b):
        if b < blocks:
            fetch(b).start()

    for c in copies[:9]:
        c.wait()
    for b in range(AHEAD):
        start(b)

    scale = gamma[...] * POINT_SCALE
    q = dot(qw[...], qall[...]).astype(BF16).astype(F32) * C ** (-0.5)
    points = rotated(qrot[...], qanc[...], dot(qpw[...], qall[...]))
    by_point = lane_sums(scale, (iota((H * PQ, H), 0) >> 2) == iota((H * PQ, H), 1))
    first, second, third = split(jnp.concatenate([2.0 * by_point * p for p in points], axis=0))
    count = qall.shape[1]
    chain = jnp.where(iota((16, count), 0) == qchain[...], 1.0, 0.0).astype(BF16)
    ones = jnp.ones((16, count), BF16)
    norms = norms_of(points, scale)
    table = jnp.concatenate(
        [q.astype(BF16), chain, chain, chain, first, second, third, *norms, ones, ones, ones], axis=0
    )

    own = iota((QB, 128), 1) == QB * lax.axis_index("col") + iota((QB, 128), 0)
    frame = jnp.zeros((QB, 128), F32)
    for k in range(12):
        value = lane_sums(qrot[k : k + 1] if k < 9 else qanc[k - 9 : k - 8], own)
        frame = jnp.where(iota((QB, 128), 1) == k, value, frame)
    aux[:, :D] = dot(jnp.where(own, 1.0, 0.0).astype(BF16), qall[...], 1, 1)
    aux[:, D:] = frame

    copies[9].wait()
    by_column = columns[:, :DEPTH]
    tall = TALL * RB
    for g in range(blocks // TALL):
        spread = dot(row_of(tall, TALL * QB * g), table, 1, 1)
        for t in range(TALL):
            at = tall * g + RB * t
            left[at : at + RB] = (spread[RB * t : RB * (t + 1)] * by_column).astype(BF16)
    copies[10].wait()
    done = 0
    for g in range(blocks // TALL):
        logits[tall * g : tall * (g + 1)] = dot(left[tall * g : tall * (g + 1)], key_side[:DEPTH])
        for _ in range(TALL // 2):
            fetch(done).wait()
            start(done + AHEAD)
            done += 1

    pick = iota((2 * H, H), 0) - iota((2 * H, H), 1)
    pick = jnp.where((pick == 0) | (pick == H), 1.0, 0.0).astype(BF16)
    turned = dot(pick, pw[...])
    upper = iota((2 * H, CZ), 0) < H
    weights = jnp.concatenate(
        [jnp.where(upper, turned, 0.0), jnp.where(upper, 0.0, turned)], axis=1
    ).astype(BF16)

    real = kmask[...] > 0
    at_head = jnp.where(head_row((RB, 128)) == iota((RB, 128), 1), 1.0, 0.0)
    lanes = [at_head] + [pltpu.roll(at_head, 16 * t, 1) for t in range(1, 4)]

    def both(b, p):
        i = QB * b + 2 * p
        return jnp.concatenate([pair[i], pair[i + 1]], axis=1)

    def bias_of(b):
        return [dot(weights, both(b, p), 1, 1) for p in range(QB // 2)]

    for b in range(blocks):
        if b >= done:
            fetch(b).wait()
            start(b + AHEAD)
        for p in range(QB // 2):
            i = QB * b + 2 * p
            logits[H * i : H * (i + 2)] += dot(weights, both(b, p), 1, 1)
    for b in range(blocks):
        at = slice(RB * b, RB * (b + 1))
        x = jnp.where(real, LOGIT_SCALE * logits[at], MASKED)
        top = jnp.max(x, axis=1, keepdims=True)
        e = jnp.exp(x - top)
        attn[at] = e.astype(BF16)
        tops = [p.astype(F32) for p in split(top)]
        extra[at] = tops[0] * lanes[0] + tops[1] * lanes[1] + tops[2] * lanes[2]
        parts = []
        for p in range(QB // 2):
            z = dot(e[2 * H * p : 2 * H * (p + 1)].astype(BF16), both(b, p))
            parts.append(jnp.where(upper, z[:, :CZ], z[:, CZ:]))
        out[b, :RB] = jnp.concatenate(parts, axis=0).astype(BF16)

    by_lane = columns[:, DEPTH:]
    own = iota((QB, RB), 1) - H * iota((QB, RB), 0)
    own = jnp.where((own >= 0) & (own < H), 1.0, 0.0).astype(BF16)
    for g in range(blocks // TALL):
        wide = dot(attn[tall * g : tall * (g + 1)], key_side[DEPTH:], 1, 1)
        for s in range(TALL):
            b = TALL * g + s
            mine = wide[RB * s : RB * (s + 1)] * by_lane
            rounded = mine.astype(BF16)
            last = mine[:, 384:] - rounded[:, 384:].astype(F32)
            rest = extra[RB * b : RB * (b + 1)] + pltpu.roll(last, 80, 1) * lanes[3]
            packed = dot(own, rounded)
            tail = dot(own, rest.astype(BF16))
            out[b, RB:] = jnp.concatenate(
                [packed[:, 128 * t : 128 * (t + 1)] for t in range(4)]
                + [tail, jnp.zeros((8, 128), F32)],
                axis=0,
            ).astype(BF16)


def finish_kernel(cols, got, w_mine, w_other, aux, out, rows, halves):
    spread = jnp.where(iota((128, WIDE), 0) == value_heads((128, WIDE)), 1.0, 0.0).astype(BF16)
    at_head = jnp.where(head_row((RB, 128)) == iota((RB, 128), 1), 1.0, 0.0)
    tail = got[:, RB:, :].astype(F32)
    count = cols * QB

    def tile(t):
        return tail[:, QB * t : QB * (t + 1)].reshape(count, 128)

    marks = tile(4)
    top = (marks + pltpu.roll(marks, 112, 1)) + pltpu.roll(marks, 96, 1)
    sums = pltpu.roll(tile(3), 32, 1) + pltpu.roll(marks, 80, 1)
    top = top.reshape(cols, QB, 128)
    factor = jnp.exp(top - jnp.max(top, axis=0, keepdims=True))
    total = jnp.sum(sums.reshape(cols, QB, 128) * factor, axis=0, keepdims=True)
    head = iota((cols, QB, 128), 2) < H
    factor = jnp.where(head, factor / total, 0.0).reshape(count, 128)
    high, low, _ = split(factor)
    wide = dot(high, spread) + dot(low, spread)
    averaged = [
        jnp.sum((tile(t) * wide[:, 128 * t : 128 * (t + 1)]).reshape(cols, QB, 128), axis=0)
        for t in range(4)
    ]
    averaged = jnp.concatenate(averaged, axis=1)

    z = jnp.zeros((RB, CZ), F32)
    for c in range(cols):
        pick = row_of(RB, QB * c)
        mine = (dot(pick, high) + dot(pick, low)) * at_head
        z = z + got[c, :RB].astype(F32) * jnp.sum(mine, axis=1, keepdims=True)
    rows[...] = z

    def mine(k):
        return aux[:, D + k : D + k + 1]

    cut = H * C
    step = H * PV
    shifted = [averaged[:, cut + step * b : cut + step * (b + 1)] - mine(9 + b) for b in range(3)]
    local = [
        mine(a) * shifted[0] + mine(3 + a) * shifted[1] + mine(6 + a) * shifted[2]
        for a in range(3)
    ]
    features = []
    for h in range(H):
        features.append(averaged[:, C * h : C * (h + 1)])
        features += [x[:, PV * h : PV * (h + 1)] for x in local]
        features.append(rows[pl.ds(h, QB, stride=H), :])
    features.append(jnp.zeros((QB, 2 * HALF - H * FEAT), F32))
    features = jnp.concatenate(features, axis=1)
    halves[0], halves[1] = features[:, :HALF], features[:, HALF:]
    core = lax.rem(lax.axis_index("row"), 2)
    mixed = dot(halves[core].astype(BF16), w_mine[...], 1, 1)
    mixed = mixed + dot(halves[1 - core].astype(BF16), w_other[...], 1, 1)
    mixed = aux[:, :D] + mixed
    centred = mixed - jnp.sum(mixed, axis=1, keepdims=True) * (1.0 / D)
    variance = jnp.sum(centred * centred, axis=1, keepdims=True) * (1.0 / D)
    normal = centred * lax.rsqrt(variance + NORM_EPS)
    width = D // cols
    out[...] = jnp.zeros(out.shape, F32)
    for c in range(cols):
        out[c, :, :width] = normal[:, width * c : width * (c + 1)]


def scale_kernel(normal, gain, shift, out):
    width = gain.shape[1]
    y = normal[...][:, :width] * gain[...] + shift[...]
    out[...] = y.T.astype(BF16)


HBM = pl.BlockSpec(memory_space=pltpu.HBM)
VMEM = pl.BlockSpec(memory_space=pltpu.VMEM)
PARAMS = pltpu.CompilerParams(vmem_limit_bytes=VMEM_BYTES)
SMALL_PARAMS = pltpu.CompilerParams(vmem_limit_bytes=16 << 20)


def shape(dims, dtype):
    return jax.ShapeDtypeStruct(dims, dtype)


def held(arrays):
    return [pltpu.VMEM(x.shape, x.dtype) for x in arrays]


def signals(count):
    return pltpu.SemaphoreType.DMA((count,))


def cost(pair, times):
    return pl.CostEstimate(
        flops=2 * times * pair.size * 128, bytes_accessed=2 * times * pair.size, transcendentals=0
    )


def pack(cols, query_single, key_single, key_rotation, key_anchor):
    own = key_single.shape[0]
    return pl.pallas_call(
        pack_kernel,
        in_specs=[HBM] * 4,
        out_specs=[VMEM, VMEM],
        out_shape=[shape((cols,) + query_single.shape, BF16), shape((own, D + 128), BF16)],
        scratch_shapes=held([query_single]) + [pltpu.VMEM((24, own), F32), signals(4)],
        compiler_params=PARAMS,
    )(query_single, key_single, key_rotation, key_anchor)


def key_parts(cols, out_weight, *small):
    keys = small[4].shape[1]
    width = out_weight.shape[0]
    results = [
        shape((cols, width, HALF), BF16),
        shape((DEPTH + WIDE, keys), BF16),
        shape((RB, DEPTH + WIDE), F32),
    ]
    return pl.pallas_call(
        key_kernel,
        in_specs=[HBM] * KEY_SMALL,
        out_specs=[HBM] * 3,
        out_shape=results,
        scratch_shapes=held((out_weight,) + small)
        + [pltpu.VMEM((width, 2 * HALF), BF16)]
        + held(results[1:])
        + [pltpu.VMEM((keys, D + 128), BF16), signals(KEY_SMALL), signals(2 + cols)],
        compiler_params=PARAMS,
        cost_estimate=pl.CostEstimate(
            flops=2 * D * keys * 1024, bytes_accessed=16 << 20, transcendentals=0
        ),
    )(out_weight, *small)


def attend(pair, *small):
    blocks, keys = pair.shape[0] // QB, pair.shape[1]
    return pl.pallas_call(
        attend_kernel,
        in_specs=[HBM] * (1 + SMALL),
        out_specs=[VMEM, VMEM],
        out_shape=[shape((blocks, CHUNK, 128), BF16), shape((QB, D + 128), F32)],
        scratch_shapes=held(small)
        + held([pair])
        + [
            pltpu.VMEM((blocks * RB, DEPTH), BF16),
            pltpu.VMEM((blocks * RB, keys), F32),
            pltpu.VMEM((blocks * RB, keys), BF16),
            pltpu.VMEM((blocks * RB, 128), F32),
            signals(blocks),
            signals(SMALL),
        ],
        compiler_params=PARAMS,
        cost_estimate=cost(pair, 3),
    )(pair, *small)


def finish(cols, *taken):
    return pl.pallas_call(
        lambda *refs: finish_kernel(cols, *refs),
        in_specs=[VMEM] * 4,
        out_specs=VMEM,
        out_shape=shape((cols, QB, 128), F32),
        scratch_shapes=[pltpu.VMEM((RB, CZ), F32), pltpu.VMEM((2, QB, HALF), F32)],
        compiler_params=SMALL_PARAMS,
    )(*taken)


def scale(*taken):
    width, queries = taken[1].shape[1], taken[0].shape[0]
    return pl.pallas_call(
        scale_kernel,
        in_specs=[VMEM] * 3,
        out_specs=VMEM,
        out_shape=shape((width, queries), BF16),
        compiler_params=SMALL_PARAMS,
    )(*taken)


def on_device(
    query_single,
    query_rotation,
    query_anchor,
    query_chain,
    key_single,
    key_rotation,
    key_anchor,
    key_chain,
    key_mask,
    pair_tile,
    query_weight,
    query_point_weight,
    key_weight,
    value_weight,
    key_point_weight,
    value_point_weight,
    pair_weight,
    head_gamma,
    chain_gap,
    out_weight,
    norm_gain,
    norm_shift,
):
    cols = lax.axis_size("col")

    def send(x):
        return lax.all_to_all(x, "col", 0, 0)

    q_pack, k_pack = pack(cols, query_single.T, key_single, key_rotation, key_anchor)
    cores = [[2 * x, 2 * x + 1] for x in range(4)]
    k_pack = lax.all_gather(k_pack, "row", axis=0, tiled=True, axis_index_groups=cores)
    k_others = [
        lax.ppermute(k_pack, "row", [(r, (r + 2 * d) % 8) for r in range(8)]) for d in (1, 2, 3)
    ]
    qall = send(q_pack).reshape(D, -1)
    gamma = head_gamma.reshape(1, -1)
    w_pack, key_side, columns = key_parts(
        cols,
        out_weight.T,
        k_pack,
        *k_others,
        key_chain.reshape(1, -1),
        key_weight.T,
        value_weight.T,
        key_point_weight.T,
        value_point_weight.T,
        gamma,
        chain_gap.reshape(1, -1),
    )
    weights = send(w_pack).reshape(D, HALF)
    parts, aux = attend(
        pair_tile,
        qall,
        query_rotation,
        query_anchor,
        query_chain.reshape(1, -1),
        query_weight.T,
        query_point_weight.T,
        gamma,
        key_mask.reshape(1, -1),
        pair_weight.T,
        columns,
        key_side,
    )
    parts, weights = lax.optimization_barrier((parts, weights))
    w_other = lax.ppermute(weights, "row", [(r, r ^ 1) for r in range(8)])
    normal = finish(cols, send(parts), weights, w_other, aux)
    normal = send(normal).reshape(-1, 128)
    return scale(normal, norm_gain.reshape(1, -1), norm_shift.reshape(1, -1)).T


def solution(mesh):
    placed = (
        P("row", "col"),
        P(None, "row"),
        P(None, "row"),
        P("row"),
        P(("col", "row"), None),
        P(None, ("col", "row")),
        P(None, ("col", "row")),
        P("col"),
        P("col"),
        P("row", "col", None),
        P(),
        P(),
        P(),
        P(),
        P(),
        P(),
        P(),
        P(),
        P(),
        P(None, "col"),
        P("col"),
        P("col"),
    )
    return jax.shard_map(
        on_device, mesh=mesh, in_specs=placed, out_specs=P("row", "col"), check_vma=False
    )
```

```python
import jax
import jax.numpy as jnp
from jax import lax
from jax.experimental import pallas as pl
from jax.experimental.pallas import tpu as pltpu
from jax.sharding import PartitionSpec as P

D = 384
H = 12
C = 16
PQ = 4
PV = 8
CZ = 128
FEAT = 168
QB = 8
RB = QB * H

LOGIT_SCALE = (1.0 / 3.0) ** 0.5
POINT_SCALE = (2.0 / (9.0 * PQ)) ** 0.5 * 0.5
NORM_EPS = 1e-05
MASKED = -1000000000.0
PRECISE = lax.Precision.HIGHEST
F32 = jnp.float32
BF16 = jnp.bfloat16

CHAIN_AT = H * C
POINTS_AT = CHAIN_AT + 3 * 16
NORMS_AT = POINTS_AT + 3 * 3 * H * PQ
DEPTH = NORMS_AT + 6 * 16
SUM_AT = H * C + 3 * H * PV
WIDE = 512
VMEM_BYTES = 63_400_000
SMALL = 11
KEY_SMALL = 12
AHEAD = 12
TALL = 8
HALF = 1024
CHUNK = RB + 48


def split(x):
    first = x.astype(BF16)
    rest = x - first.astype(F32)
    second = rest.astype(BF16)
    third = (rest - second.astype(F32)).astype(BF16)
    return first, second, third


def dot(a, b, ca=1, cb=0, precision=None):
    return lax.dot_general(
        a, b, (((ca,), (cb,)), ((), ())), precision=precision, preferred_element_type=F32
    )


def iota(shape, axis):
    return lax.broadcasted_iota(jnp.int32, shape, axis)


def head_row(shape_):
    row = iota(shape_, 0)
    return row - H * ((row * 43) >> 9)


def column_heads():
    k = iota((RB, DEPTH), 1)
    point = k - POINTS_AT
    for _ in range(8):
        point = jnp.where(point >= H * PQ, point - H * PQ, point)
    of_chain = jnp.where(k < POINTS_AT, -1, point >> 2)
    return jnp.where(k < CHAIN_AT, k >> 4, jnp.where(k < NORMS_AT, of_chain, (k - NORMS_AT) & 15))


def value_heads(shape_):
    f = iota(shape_, 1)
    point = f - H * C
    for _ in range(2):
        point = jnp.where(point >= H * PV, point - H * PV, point)
    return jnp.where(f < H * C, f >> 4, jnp.where(f < SUM_AT, point >> 3, f - SUM_AT))


def row_of(rows, first):
    gap = iota((rows, 128), 0) - H * (iota((rows, 128), 1) - first)
    return jnp.where((gap >= 0) & (gap < H), 1.0, 0.0).astype(BF16)


def fetch_all(pairs, sems):
    copies = [pltpu.make_async_copy(src, dst, sems.at[k]) for k, (src, dst) in enumerate(pairs)]
    for c in copies:
        c.start()
    return copies


def pack_kernel(qs_in, ks_in, krot_in, kanc_in, q_out, k_out, qs, frames, sems):
    own = ks_in.shape[0]
    copies = fetch_all(
        [
            (krot_in, frames.at[pl.ds(0, 9)]),
            (kanc_in, frames.at[pl.ds(16, 3)]),
            (qs_in, qs),
            (ks_in, k_out.at[:, pl.ds(0, D)]),
        ],
        sems,
    )
    copies[0].wait()
    copies[1].wait()
    row = iota((24, own), 0)
    both = jnp.where((row < 9) | ((row >= 16) & (row < 19)), frames[...], 0.0)
    parts = [p.astype(F32) for p in split(both)]
    parts = jnp.concatenate(parts + [jnp.zeros((56, own), F32)], axis=0)
    k_out[:, D:] = parts.T.astype(BF16)
    copies[2].wait()
    for c in range(q_out.shape[0]):
        q_out[c] = qs[...]
    copies[3].wait()


def rotated(rot, anc, local):
    size = local.shape[0] // 3
    part = [local[size * b : size * (b + 1)] for b in range(3)]
    return [
        rot[3 * a : 3 * a + 1] * part[0]
        + rot[3 * a + 1 : 3 * a + 2] * part[1]
        + rot[3 * a + 2 : 3 * a + 3] * part[2]
        + anc[a : a + 1]
        for a in range(3)
    ]


def lane_sums(table, wanted):
    return jnp.sum(jnp.where(wanted, table, 0.0), axis=1, keepdims=True)


def norms_of(points, scale):
    heads = jnp.where(iota((16, H * PQ), 0) == (iota((16, H * PQ), 1) >> 2), 1.0, 0.0)
    by_head = lane_sums(scale, iota((16, H), 0) == iota((16, H), 1))
    squares = points[0] * points[0] + points[1] * points[1] + points[2] * points[2]
    return split(-by_head * dot(heads, squares, precision=PRECISE))


def key_kernel(*refs):
    small_hbm, (w_out, key_out, column_out) = refs[:KEY_SMALL], refs[KEY_SMALL : KEY_SMALL + 3]
    small = refs[KEY_SMALL + 3 : 2 * KEY_SMALL + 3]
    w_pad, key_side, columns, kall, sems, more = refs[2 * KEY_SMALL + 3 :]
    copies = fetch_all(list(zip(small_hbm, small)), sems)
    for c in copies:
        c.wait()
    w, k0, k1, k2, k3, kchain, kw, vw, kpw, vpw, gamma, gap = small
    half = w_pad.shape[1] // 2
    width = w.shape[1]
    w_pad[:, :width] = w[...]
    w_pad[:, width:] = jnp.zeros((w.shape[0], 2 * half - width), BF16)
    core = lax.rem(lax.axis_index("row"), 2)
    mine = pl.ds(pl.multiple_of(core * half, half), half)
    cols = w_out.shape[0]
    stores = fetch_all([(w_pad.at[:, mine], w_out.at[c]) for c in range(cols)], more)

    chips = 4
    here = lax.axis_index("row") // 2
    size = k0.shape[0]
    for d, block in enumerate((k0, k1, k2, k3)):
        at = pl.multiple_of(lax.rem(here + chips - d, chips) * size, size)
        kall[pl.ds(at, size), :] = block[...]

    rows = kall[:, :D]
    keys = kall.shape[0]
    eye = jnp.where(iota((128, 128), 0) == iota((128, 128), 1), 1.0, 0.0).astype(BF16)
    frames = dot(eye, kall[:, D:], 1, 1)
    frames = (frames[0:24] + frames[24:48]) + frames[48:72]
    krot, kanc = frames[0:9], frames[16:19]

    def project(weight):
        return dot(weight[...], rows, 1, 1)

    kpoints = [p.astype(BF16) for p in rotated(krot, kanc, project(kpw))]
    vpoints = [p.astype(BF16) for p in rotated(krot, kanc, project(vpw))]
    apart = jnp.where(iota((16, keys), 0) != kchain[...], 1.0, 0.0).astype(BF16)
    ones = jnp.ones((16, keys), BF16)
    norms = norms_of([p.astype(F32) for p in kpoints], gamma[...] * POINT_SCALE)
    pieces = [project(kw).astype(BF16), apart, apart, apart, *kpoints, *kpoints, *kpoints]
    pieces += [ones, ones, ones, *norms]
    pieces += [project(vw).astype(BF16), *vpoints, ones, jnp.zeros((16, keys), BF16)]
    at = 0
    for piece in pieces:
        key_side[at : at + piece.shape[0]] = piece
        at += piece.shape[0]

    own_gap = lane_sums(gap[...], head_row((RB, H)) == iota((RB, H), 1))
    lane = iota((RB, DEPTH), 1)
    by_column = jnp.where(head_row((RB, DEPTH)) == column_heads(), 1.0, 0.0)
    for t, part in enumerate(split(own_gap)):
        inside = (lane >= CHAIN_AT + 16 * t) & (lane < CHAIN_AT + 16 * (t + 1))
        by_column = jnp.where(inside, part.astype(F32), by_column)
    columns[:, :DEPTH] = by_column
    columns[:, DEPTH:] = jnp.where(head_row((RB, WIDE)) == value_heads((RB, WIDE)), 1.0, 0.0)
    stores.append(pltpu.make_async_copy(key_side, key_out, more.at[cols]))
    stores.append(pltpu.make_async_copy(columns, column_out, more.at[cols + 1]))
    stores[cols].start()
    stores[cols + 1].start()

    for c in stores:
        c.wait()


def attend_kernel(pair_hbm, *refs):
    small_hbm, (out, aux), small = refs[:SMALL], refs[SMALL : SMALL + 2], refs[SMALL + 2 : 2 * SMALL + 2]
    pair, left, logits, bias, attn, extra, pair_sems, sems = refs[2 * SMALL + 2 :]
    pw, qall, qrot, qanc, qchain, qw, qpw, gamma, kmask, columns, key_side = small
    blocks = pair.shape[0] // QB
    copies = fetch_all(list(zip(small_hbm, small))[:1], sems)

    def fetch(b):
        at = pl.ds(QB * b, QB)
        return pltpu.make_async_copy(pair_hbm.at[at], pair.at[at], pair_sems.at[b])

    def start(b):
        if b < blocks:
            fetch(b).start()

    for b in range(AHEAD):
        start(b)
    copies += fetch_all(list(zip(small_hbm, small))[1:], sems.at[pl.ds(1, SMALL - 1)])
    copies[0].wait()

    pick = iota((2 * H, H), 0) - iota((2 * H, H), 1)
    pick = jnp.where((pick == 0) | (pick == H), 1.0, 0.0).astype(BF16)
    turned = dot(pick, pw[...])
    upper = iota((2 * H, CZ), 0) < H
    weights = jnp.concatenate(
        [jnp.where(upper, turned, 0.0), jnp.where(upper, 0.0, turned)], axis=1
    ).astype(BF16)

    def both(b, p):
        i = QB * b + 2 * p
        return jnp.concatenate([pair[i], pair[i + 1]], axis=1)

    for b in range(blocks):
        fetch(b).wait()
        start(b + AHEAD)
        for p in range(QB // 2):
            i = QB * b + 2 * p
            bias[H * i : H * (i + 2)] = dot(weights, both(b, p), 1, 1)

    for c in copies[1:]:
        c.wait()

    scale = gamma[...] * POINT_SCALE
    q = dot(qw[...], qall[...]).astype(BF16).astype(F32) * C ** (-0.5)
    points = rotated(qrot[...], qanc[...], dot(qpw[...], qall[...]))
    by_point = lane_sums(scale, (iota((H * PQ, H), 0) >> 2) == iota((H * PQ, H), 1))
    first, second, third = split(jnp.concatenate([2.0 * by_point * p for p in points], axis=0))
    count = qall.shape[1]
    chain = jnp.where(iota((16, count), 0) == qchain[...], 1.0, 0.0).astype(BF16)
    ones = jnp.ones((16, count), BF16)
    norms = norms_of(points, scale)
    table = jnp.concatenate(
        [q.astype(BF16), chain, chain, chain, first, second, third, *norms, ones, ones, ones], axis=0
    )

    own = iota((QB, 128), 1) == QB * lax.axis_index("col") + iota((QB, 128), 0)
    frame = jnp.zeros((QB, 128), F32)
    for k in range(12):
        value = lane_sums(qrot[k : k + 1] if k < 9 else qanc[k - 9 : k - 8], own)
        frame = jnp.where(iota((QB, 128), 1) == k, value, frame)
    aux[:, :D] = dot(jnp.where(own, 1.0, 0.0).astype(BF16), qall[...], 1, 1)
    aux[:, D:] = frame

    by_column = columns[:, :DEPTH]
    tall = TALL * RB
    for g in range(blocks // TALL):
        spread = dot(row_of(tall, TALL * QB * g), table, 1, 1)
        for t in range(TALL):
            at = tall * g + RB * t
            left[at : at + RB] = (spread[RB * t : RB * (t + 1)] * by_column).astype(BF16)
    for g in range(blocks // TALL):
        logits[tall * g : tall * (g + 1)] = dot(left[tall * g : tall * (g + 1)], key_side[:DEPTH])

    real = kmask[...] > 0
    at_head = jnp.where(head_row((RB, 128)) == iota((RB, 128), 1), 1.0, 0.0)
    lanes = [at_head] + [pltpu.roll(at_head, 16 * t, 1) for t in range(1, 4)]

    def weigh(b):
        at = slice(RB * b, RB * (b + 1))
        x = jnp.where(real, LOGIT_SCALE * (logits[at] + bias[at]), MASKED)
        top = jnp.max(x, axis=1, keepdims=True)
        e = jnp.exp(x - top)
        attn[at] = e.astype(BF16)
        tops = [p.astype(F32) for p in split(top)]
        extra[at] = tops[0] * lanes[0] + tops[1] * lanes[1] + tops[2] * lanes[2]
        return [e[2 * H * p : 2 * H * (p + 1)].astype(BF16) for p in range(QB // 2)]

    e = weigh(0)
    for b in range(blocks):
        later = weigh(b + 1) if b + 1 < blocks else None
        parts = []
        for p in range(QB // 2):
            z = dot(e[p], both(b, p))
            parts.append(jnp.where(upper, z[:, :CZ], z[:, CZ:]))
        out[b, :RB] = jnp.concatenate(parts, axis=0).astype(BF16)
        e = later

    by_lane = columns[:, DEPTH:]
    own = iota((QB, RB), 1) - H * iota((QB, RB), 0)
    own = jnp.where((own >= 0) & (own < H), 1.0, 0.0).astype(BF16)
    for g in range(blocks // TALL):
        wide = dot(attn[tall * g : tall * (g + 1)], key_side[DEPTH:], 1, 1)
        for s in range(TALL):
            b = TALL * g + s
            mine = wide[RB * s : RB * (s + 1)] * by_lane
            rounded = mine.astype(BF16)
            last = mine[:, 384:] - rounded[:, 384:].astype(F32)
            rest = extra[RB * b : RB * (b + 1)] + pltpu.roll(last, 80, 1) * lanes[3]
            packed = dot(own, rounded)
            tail = dot(own, rest.astype(BF16))
            out[b, RB:] = jnp.concatenate(
                [packed[:, 128 * t : 128 * (t + 1)] for t in range(4)]
                + [tail, jnp.zeros((8, 128), F32)],
                axis=0,
            ).astype(BF16)


def finish_kernel(cols, got, w_mine, w_other, aux, out, rows, halves):
    spread = jnp.where(iota((128, WIDE), 0) == value_heads((128, WIDE)), 1.0, 0.0).astype(BF16)
    at_head = jnp.where(head_row((RB, 128)) == iota((RB, 128), 1), 1.0, 0.0)
    tail = got[:, RB:, :].astype(F32)
    count = cols * QB

    def tile(t):
        return tail[:, QB * t : QB * (t + 1)].reshape(count, 128)

    marks = tile(4)
    top = (marks + pltpu.roll(marks, 112, 1)) + pltpu.roll(marks, 96, 1)
    sums = pltpu.roll(tile(3), 32, 1) + pltpu.roll(marks, 80, 1)
    top = top.reshape(cols, QB, 128)
    factor = jnp.exp(top - jnp.max(top, axis=0, keepdims=True))
    total = jnp.sum(sums.reshape(cols, QB, 128) * factor, axis=0, keepdims=True)
    head = iota((cols, QB, 128), 2) < H
    factor = jnp.where(head, factor / total, 0.0).reshape(count, 128)
    high, low, _ = split(factor)
    wide = dot(high, spread) + dot(low, spread)
    averaged = [
        jnp.sum((tile(t) * wide[:, 128 * t : 128 * (t + 1)]).reshape(cols, QB, 128), axis=0)
        for t in range(4)
    ]
    averaged = jnp.concatenate(averaged, axis=1)

    z = jnp.zeros((RB, CZ), F32)
    for c in range(cols):
        pick = row_of(RB, QB * c)
        mine = (dot(pick, high) + dot(pick, low)) * at_head
        z = z + got[c, :RB].astype(F32) * jnp.sum(mine, axis=1, keepdims=True)
    rows[...] = z

    def mine(k):
        return aux[:, D + k : D + k + 1]

    cut = H * C
    step = H * PV
    shifted = [averaged[:, cut + step * b : cut + step * (b + 1)] - mine(9 + b) for b in range(3)]
    local = [
        mine(a) * shifted[0] + mine(3 + a) * shifted[1] + mine(6 + a) * shifted[2]
        for a in range(3)
    ]
    features = []
    for h in range(H):
        features.append(averaged[:, C * h : C * (h + 1)])
        features += [x[:, PV * h : PV * (h + 1)] for x in local]
        features.append(rows[pl.ds(h, QB, stride=H), :])
    features.append(jnp.zeros((QB, 2 * HALF - H * FEAT), F32))
    features = jnp.concatenate(features, axis=1)
    halves[0], halves[1] = features[:, :HALF], features[:, HALF:]
    core = lax.rem(lax.axis_index("row"), 2)
    mixed = dot(halves[core].astype(BF16), w_mine[...], 1, 1)
    mixed = mixed + dot(halves[1 - core].astype(BF16), w_other[...], 1, 1)
    mixed = aux[:, :D] + mixed
    centred = mixed - jnp.sum(mixed, axis=1, keepdims=True) * (1.0 / D)
    variance = jnp.sum(centred * centred, axis=1, keepdims=True) * (1.0 / D)
    normal = centred * lax.rsqrt(variance + NORM_EPS)
    width = D // cols
    out[...] = jnp.zeros(out.shape, F32)
    for c in range(cols):
        out[c, :, :width] = normal[:, width * c : width * (c + 1)]


def scale_kernel(normal, gain, shift, out):
    width = gain.shape[1]
    y = normal[...][:, :width] * gain[...] + shift[...]
    out[...] = y.T.astype(BF16)


HBM = pl.BlockSpec(memory_space=pltpu.HBM)
VMEM = pl.BlockSpec(memory_space=pltpu.VMEM)
PARAMS = pltpu.CompilerParams(vmem_limit_bytes=VMEM_BYTES)
SMALL_PARAMS = pltpu.CompilerParams(vmem_limit_bytes=16 << 20)


def shape(dims, dtype):
    return jax.ShapeDtypeStruct(dims, dtype)


def held(arrays):
    return [pltpu.VMEM(x.shape, x.dtype) for x in arrays]


def signals(count):
    return pltpu.SemaphoreType.DMA((count,))


def cost(pair, times):
    return pl.CostEstimate(
        flops=2 * times * pair.size * 128, bytes_accessed=2 * times * pair.size, transcendentals=0
    )


def pack(cols, query_single, key_single, key_rotation, key_anchor):
    own = key_single.shape[0]
    return pl.pallas_call(
        pack_kernel,
        in_specs=[HBM] * 4,
        out_specs=[VMEM, VMEM],
        out_shape=[shape((cols,) + query_single.shape, BF16), shape((own, D + 128), BF16)],
        scratch_shapes=held([query_single]) + [pltpu.VMEM((24, own), F32), signals(4)],
        compiler_params=PARAMS,
    )(query_single, key_single, key_rotation, key_anchor)


def key_parts(cols, out_weight, *small):
    keys = small[4].shape[1]
    width = out_weight.shape[0]
    results = [
        shape((cols, width, HALF), BF16),
        shape((DEPTH + WIDE, keys), BF16),
        shape((RB, DEPTH + WIDE), F32),
    ]
    return pl.pallas_call(
        key_kernel,
        in_specs=[HBM] * KEY_SMALL,
        out_specs=[HBM] * 3,
        out_shape=results,
        scratch_shapes=held((out_weight,) + small)
        + [pltpu.VMEM((width, 2 * HALF), BF16)]
        + held(results[1:])
        + [pltpu.VMEM((keys, D + 128), BF16), signals(KEY_SMALL), signals(2 + cols)],
        compiler_params=PARAMS,
        cost_estimate=pl.CostEstimate(
            flops=2 * D * keys * 1024, bytes_accessed=16 << 20, transcendentals=0
        ),
    )(out_weight, *small)


def attend(pair, *small):
    blocks, keys = pair.shape[0] // QB, pair.shape[1]
    return pl.pallas_call(
        attend_kernel,
        in_specs=[HBM] * (1 + SMALL),
        out_specs=[VMEM, VMEM],
        out_shape=[shape((blocks, CHUNK, 128), BF16), shape((QB, D + 128), F32)],
        scratch_shapes=held(small)
        + held([pair])
        + [
            pltpu.VMEM((blocks * RB, DEPTH), BF16),
            pltpu.VMEM((blocks * RB, keys), F32),
            pltpu.VMEM((blocks * RB, keys), F32),
            pltpu.VMEM((blocks * RB, keys), BF16),
            pltpu.VMEM((blocks * RB, 128), F32),
            signals(blocks),
            signals(SMALL),
        ],
        compiler_params=PARAMS,
        cost_estimate=cost(pair, 3),
    )(pair, *small)


def finish(cols, *taken):
    return pl.pallas_call(
        lambda *refs: finish_kernel(cols, *refs),
        in_specs=[VMEM] * 4,
        out_specs=VMEM,
        out_shape=shape((cols, QB, 128), F32),
        scratch_shapes=[pltpu.VMEM((RB, CZ), F32), pltpu.VMEM((2, QB, HALF), F32)],
        compiler_params=SMALL_PARAMS,
    )(*taken)


def scale(*taken):
    width, queries = taken[1].shape[1], taken[0].shape[0]
    return pl.pallas_call(
        scale_kernel,
        in_specs=[VMEM] * 3,
        out_specs=VMEM,
        out_shape=shape((width, queries), BF16),
        compiler_params=SMALL_PARAMS,
    )(*taken)


def on_device(
    query_single,
    query_rotation,
    query_anchor,
    query_chain,
    key_single,
    key_rotation,
    key_anchor,
    key_chain,
    key_mask,
    pair_tile,
    query_weight,
    query_point_weight,
    key_weight,
    value_weight,
    key_point_weight,
    value_point_weight,
    pair_weight,
    head_gamma,
    chain_gap,
    out_weight,
    norm_gain,
    norm_shift,
):
    cols = lax.axis_size("col")

    def send(x):
        return lax.all_to_all(x, "col", 0, 0)

    q_pack, k_pack = pack(cols, query_single.T, key_single, key_rotation, key_anchor)
    cores = [[2 * x, 2 * x + 1] for x in range(4)]
    k_pack = lax.all_gather(k_pack, "row", axis=0, tiled=True, axis_index_groups=cores)
    k_others = [
        lax.ppermute(k_pack, "row", [(r, (r + 2 * d) % 8) for r in range(8)]) for d in (1, 2, 3)
    ]
    qall = send(q_pack).reshape(D, -1)
    gamma = head_gamma.reshape(1, -1)
    w_pack, key_side, columns = key_parts(
        cols,
        out_weight.T,
        k_pack,
        *k_others,
        key_chain.reshape(1, -1),
        key_weight.T,
        value_weight.T,
        key_point_weight.T,
        value_point_weight.T,
        gamma,
        chain_gap.reshape(1, -1),
    )
    weights = send(w_pack).reshape(D, HALF)
    parts, aux = attend(
        pair_tile,
        pair_weight.T,
        qall,
        query_rotation,
        query_anchor,
        query_chain.reshape(1, -1),
        query_weight.T,
        query_point_weight.T,
        gamma,
        key_mask.reshape(1, -1),
        columns,
        key_side,
    )
    parts, weights = lax.optimization_barrier((parts, weights))
    w_other = lax.ppermute(weights, "row", [(r, r ^ 1) for r in range(8)])
    normal = finish(cols, send(parts), weights, w_other, aux)
    normal = send(normal).reshape(-1, 128)
    return scale(normal, norm_gain.reshape(1, -1), norm_shift.reshape(1, -1)).T


def solution(mesh):
    placed = (
        P("row", "col"),
        P(None, "row"),
        P(None, "row"),
        P("row"),
        P(("col", "row"), None),
        P(None, ("col", "row")),
        P(None, ("col", "row")),
        P("col"),
        P("col"),
        P("row", "col", None),
        P(),
        P(),
        P(),
        P(),
        P(),
        P(),
        P(),
        P(),
        P(),
        P(None, "col"),
        P("col"),
        P("col"),
    )
    return jax.shard_map(
        on_device, mesh=mesh, in_specs=placed, out_specs=P("row", "col"), check_vma=False
    )
```

```python
import jax
import jax.numpy as jnp
from jax import lax
from jax.experimental import pallas as pl
from jax.experimental.pallas import tpu as pltpu
from jax.sharding import PartitionSpec as P

D = 384
H = 12
C = 16
PQ = 4
PV = 8
CZ = 128
FEAT = 168
QB = 8
RB = QB * H

LOGIT_SCALE = (1.0 / 3.0) ** 0.5
POINT_SCALE = (2.0 / (9.0 * PQ)) ** 0.5 * 0.5
NORM_EPS = 1e-05
MASKED = -1000000000.0
PRECISE = lax.Precision.HIGHEST
F32 = jnp.float32
BF16 = jnp.bfloat16

CHAIN_AT = H * C
POINTS_AT = CHAIN_AT + 3 * 16
NORMS_AT = POINTS_AT + 3 * 3 * H * PQ
DEPTH = NORMS_AT + 6 * 16
SUM_AT = H * C + 3 * H * PV
WIDE = 512
VMEM_BYTES = 63_400_000
SMALL = 11
KEY_SMALL = 12
AHEAD = 12
TALL = 8
HALF = 1024
CHUNK = RB + 48


def split(x):
    first = x.astype(BF16)
    rest = x - first.astype(F32)
    second = rest.astype(BF16)
    third = (rest - second.astype(F32)).astype(BF16)
    return first, second, third


def dot(a, b, ca=1, cb=0, precision=None):
    return lax.dot_general(
        a, b, (((ca,), (cb,)), ((), ())), precision=precision, preferred_element_type=F32
    )


def iota(shape, axis):
    return lax.broadcasted_iota(jnp.int32, shape, axis)


def head_row(shape_):
    row = iota(shape_, 0)
    return row - H * ((row * 43) >> 9)


def column_heads():
    k = iota((RB, DEPTH), 1)
    point = k - POINTS_AT
    for _ in range(8):
        point = jnp.where(point >= H * PQ, point - H * PQ, point)
    of_chain = jnp.where(k < POINTS_AT, -1, point >> 2)
    return jnp.where(k < CHAIN_AT, k >> 4, jnp.where(k < NORMS_AT, of_chain, (k - NORMS_AT) & 15))


def value_heads(shape_):
    f = iota(shape_, 1)
    point = f - H * C
    for _ in range(2):
        point = jnp.where(point >= H * PV, point - H * PV, point)
    return jnp.where(f < H * C, f >> 4, jnp.where(f < SUM_AT, point >> 3, f - SUM_AT))


def row_of(rows, first):
    gap = iota((rows, 128), 0) - H * (iota((rows, 128), 1) - first)
    return jnp.where((gap >= 0) & (gap < H), 1.0, 0.0).astype(BF16)


def fetch_all(pairs, sems):
    copies = [pltpu.make_async_copy(src, dst, sems.at[k]) for k, (src, dst) in enumerate(pairs)]
    for c in copies:
        c.start()
    return copies


def pack_kernel(qs_in, ks_in, krot_in, kanc_in, q_out, k_out, qs, frames, sems):
    own = ks_in.shape[0]
    copies = fetch_all(
        [
            (krot_in, frames.at[pl.ds(0, 9)]),
            (kanc_in, frames.at[pl.ds(16, 3)]),
            (qs_in, qs),
            (ks_in, k_out.at[:, pl.ds(0, D)]),
        ],
        sems,
    )
    copies[0].wait()
    copies[1].wait()
    row = iota((24, own), 0)
    both = jnp.where((row < 9) | ((row >= 16) & (row < 19)), frames[...], 0.0)
    parts = [p.astype(F32) for p in split(both)]
    parts = jnp.concatenate(parts + [jnp.zeros((56, own), F32)], axis=0)
    k_out[:, D:] = parts.T.astype(BF16)
    copies[2].wait()
    for c in range(q_out.shape[0]):
        q_out[c] = qs[...].astype(BF16)
    copies[3].wait()


def rotated(rot, anc, local):
    size = local.shape[0] // 3
    part = [local[size * b : size * (b + 1)] for b in range(3)]
    return [
        rot[3 * a : 3 * a + 1] * part[0]
        + rot[3 * a + 1 : 3 * a + 2] * part[1]
        + rot[3 * a + 2 : 3 * a + 3] * part[2]
        + anc[a : a + 1]
        for a in range(3)
    ]


def lane_sums(table, wanted):
    return jnp.sum(jnp.where(wanted, table, 0.0), axis=1, keepdims=True)


def norms_of(points, scale):
    heads = jnp.where(iota((16, H * PQ), 0) == (iota((16, H * PQ), 1) >> 2), 1.0, 0.0)
    by_head = lane_sums(scale, iota((16, H), 0) == iota((16, H), 1))
    squares = points[0] * points[0] + points[1] * points[1] + points[2] * points[2]
    return split(-by_head * dot(heads, squares, precision=PRECISE))


def key_kernel(*refs):
    small_hbm, (w_out, key_out, column_out) = refs[:KEY_SMALL], refs[KEY_SMALL : KEY_SMALL + 3]
    small = refs[KEY_SMALL + 3 : 2 * KEY_SMALL + 3]
    w_pad, key_side, columns, kall, sems, more = refs[2 * KEY_SMALL + 3 :]
    copies = fetch_all(list(zip(small_hbm, small)), sems)
    for c in copies:
        c.wait()
    w, k0, k1, k2, k3, kchain, kw, vw, kpw, vpw, gamma, gap = small
    half = w_pad.shape[1] // 2
    width = w.shape[1]
    w_pad[:, :width] = w[...].astype(BF16)
    w_pad[:, width:] = jnp.zeros((w.shape[0], 2 * half - width), BF16)
    core = lax.rem(lax.axis_index("row"), 2)
    mine = pl.ds(pl.multiple_of(core * half, half), half)
    cols = w_out.shape[0]
    half_weights = w_pad[:, mine]
    for c in range(cols):
        w_out[c] = half_weights

    chips = 4
    here = lax.axis_index("row") // 2
    size = k0.shape[0]
    for d, block in enumerate((k0, k1, k2, k3)):
        at = pl.multiple_of(lax.rem(here + chips - d, chips) * size, size)
        kall[pl.ds(at, size), :] = block[...]

    rows = kall[:, :D]
    keys = kall.shape[0]
    eye = jnp.where(iota((128, 128), 0) == iota((128, 128), 1), 1.0, 0.0).astype(BF16)
    frames = dot(eye, kall[:, D:], 1, 1)
    frames = (frames[0:24] + frames[24:48]) + frames[48:72]
    krot, kanc = frames[0:9], frames[16:19]

    def project(weight):
        return dot(weight[...], rows, 1, 1)

    kpoints = [p.astype(BF16) for p in rotated(krot, kanc, project(kpw))]
    vpoints = [p.astype(BF16) for p in rotated(krot, kanc, project(vpw))]
    apart = jnp.where(iota((16, keys), 0) != kchain[...], 1.0, 0.0).astype(BF16)
    ones = jnp.ones((16, keys), BF16)
    norms = norms_of([p.astype(F32) for p in kpoints], gamma[...] * POINT_SCALE)
    pieces = [project(kw).astype(BF16), apart, apart, apart, *kpoints, *kpoints, *kpoints]
    pieces += [ones, ones, ones, *norms]
    pieces += [project(vw).astype(BF16), *vpoints, ones, jnp.zeros((16, keys), BF16)]
    at = 0
    for piece in pieces:
        key_side[at : at + piece.shape[0]] = piece
        at += piece.shape[0]

    own_gap = lane_sums(gap[...], head_row((RB, H)) == iota((RB, H), 1))
    lane = iota((RB, DEPTH), 1)
    by_column = jnp.where(head_row((RB, DEPTH)) == column_heads(), 1.0, 0.0)
    for t, part in enumerate(split(own_gap)):
        inside = (lane >= CHAIN_AT + 16 * t) & (lane < CHAIN_AT + 16 * (t + 1))
        by_column = jnp.where(inside, part.astype(F32), by_column)
    columns[:, :DEPTH] = by_column
    columns[:, DEPTH:] = jnp.where(head_row((RB, WIDE)) == value_heads((RB, WIDE)), 1.0, 0.0)
    stores = fetch_all([(key_side, key_out), (columns, column_out)], more)
    for c in stores:
        c.wait()


def attend_kernel(pair_hbm, *refs):
    small_hbm, (out, aux), small = refs[:SMALL], refs[SMALL : SMALL + 2], refs[SMALL + 2 : 2 * SMALL + 2]
    pair, left, logits, bias, attn, extra, pair_sems, sems = refs[2 * SMALL + 2 :]
    pw, qall, qrot, qanc, qchain, qw, qpw, gamma, kmask, columns, key_side = small
    blocks = pair.shape[0] // QB
    copies = fetch_all(list(zip(small_hbm, small))[:1], sems)

    def fetch(b):
        at = pl.ds(QB * b, QB)
        return pltpu.make_async_copy(pair_hbm.at[at], pair.at[at], pair_sems.at[b])

    def start(b):
        if b < blocks:
            fetch(b).start()

    for b in range(AHEAD):
        start(b)
    copies += fetch_all(list(zip(small_hbm, small))[1:], sems.at[pl.ds(1, SMALL - 1)])
    copies[0].wait()

    pick = iota((2 * H, H), 0) - iota((2 * H, H), 1)
    pick = jnp.where((pick == 0) | (pick == H), 1.0, 0.0).astype(BF16)
    turned = dot(pick, pw[...].astype(BF16))
    upper = iota((2 * H, CZ), 0) < H
    weights = jnp.concatenate(
        [jnp.where(upper, turned, 0.0), jnp.where(upper, 0.0, turned)], axis=1
    ).astype(BF16)

    def both(b, p):
        i = QB * b + 2 * p
        return jnp.concatenate([pair[i], pair[i + 1]], axis=1)

    for b in range(blocks):
        fetch(b).wait()
        start(b + AHEAD)
        for p in range(QB // 2):
            i = QB * b + 2 * p
            bias[H * i : H * (i + 2)] = dot(weights, both(b, p), 1, 1)

    for c in copies[1:]:
        c.wait()

    scale = gamma[...] * POINT_SCALE
    q = dot(qw[...], qall[...]).astype(BF16).astype(F32) * C ** (-0.5)
    points = rotated(qrot[...], qanc[...], dot(qpw[...], qall[...]))
    by_point = lane_sums(scale, (iota((H * PQ, H), 0) >> 2) == iota((H * PQ, H), 1))
    first, second, third = split(jnp.concatenate([2.0 * by_point * p for p in points], axis=0))
    count = qall.shape[1]
    chain = jnp.where(iota((16, count), 0) == qchain[...], 1.0, 0.0).astype(BF16)
    ones = jnp.ones((16, count), BF16)
    norms = norms_of(points, scale)
    table = jnp.concatenate(
        [q.astype(BF16), chain, chain, chain, first, second, third, *norms, ones, ones, ones], axis=0
    )

    own = iota((QB, 128), 1) == QB * lax.axis_index("col") + iota((QB, 128), 0)
    frame = jnp.zeros((QB, 128), F32)
    for k in range(12):
        value = lane_sums(qrot[k : k + 1] if k < 9 else qanc[k - 9 : k - 8], own)
        frame = jnp.where(iota((QB, 128), 1) == k, value, frame)
    aux[:, :D] = dot(jnp.where(own, 1.0, 0.0).astype(BF16), qall[...], 1, 1)
    aux[:, D:] = frame

    by_column = columns[:, :DEPTH]
    tall = TALL * RB
    for g in range(blocks // TALL):
        spread = dot(row_of(tall, TALL * QB * g), table, 1, 1)
        for t in range(TALL):
            at = tall * g + RB * t
            left[at : at + RB] = (spread[RB * t : RB * (t + 1)] * by_column).astype(BF16)
    for g in range(blocks // TALL):
        logits[tall * g : tall * (g + 1)] = dot(left[tall * g : tall * (g + 1)], key_side[:DEPTH])

    real = kmask[...] > 0
    at_head = jnp.where(head_row((RB, 128)) == iota((RB, 128), 1), 1.0, 0.0)
    lanes = [at_head] + [pltpu.roll(at_head, 16 * t, 1) for t in range(1, 4)]

    def weigh(b):
        at = slice(RB * b, RB * (b + 1))
        x = jnp.where(real, LOGIT_SCALE * (logits[at] + bias[at]), MASKED)
        top = jnp.max(x, axis=1, keepdims=True)
        e = jnp.exp(x - top)
        attn[at] = e.astype(BF16)
        tops = [p.astype(F32) for p in split(top)]
        extra[at] = tops[0] * lanes[0] + tops[1] * lanes[1] + tops[2] * lanes[2]
        return [e[2 * H * p : 2 * H * (p + 1)].astype(BF16) for p in range(QB // 2)]

    e = weigh(0)
    for b in range(blocks):
        later = weigh(b + 1) if b + 1 < blocks else None
        parts = []
        for p in range(QB // 2):
            z = dot(e[p], both(b, p))
            parts.append(jnp.where(upper, z[:, :CZ], z[:, CZ:]))
        out[b, :RB] = jnp.concatenate(parts, axis=0).astype(BF16)
        e = later

    by_lane = columns[:, DEPTH:]
    own = iota((QB, RB), 1) - H * iota((QB, RB), 0)
    own = jnp.where((own >= 0) & (own < H), 1.0, 0.0).astype(BF16)
    for g in range(blocks // TALL):
        wide = dot(attn[tall * g : tall * (g + 1)], key_side[DEPTH:], 1, 1)
        for s in range(TALL):
            b = TALL * g + s
            mine = wide[RB * s : RB * (s + 1)] * by_lane
            rounded = mine.astype(BF16)
            last = mine[:, 384:] - rounded[:, 384:].astype(F32)
            rest = extra[RB * b : RB * (b + 1)] + pltpu.roll(last, 80, 1) * lanes[3]
            packed = dot(own, rounded)
            tail = dot(own, rest.astype(BF16))
            out[b, RB:] = jnp.concatenate(
                [packed[:, 128 * t : 128 * (t + 1)] for t in range(4)]
                + [tail, jnp.zeros((8, 128), F32)],
                axis=0,
            ).astype(BF16)


def finish_kernel(cols, got, w_mine, w_other, aux, out, rows, halves):
    spread = jnp.where(iota((128, WIDE), 0) == value_heads((128, WIDE)), 1.0, 0.0).astype(BF16)
    at_head = jnp.where(head_row((RB, 128)) == iota((RB, 128), 1), 1.0, 0.0)
    tail = got[:, RB:, :].astype(F32)
    count = cols * QB

    def tile(t):
        return tail[:, QB * t : QB * (t + 1)].reshape(count, 128)

    marks = tile(4)
    top = (marks + pltpu.roll(marks, 112, 1)) + pltpu.roll(marks, 96, 1)
    sums = pltpu.roll(tile(3), 32, 1) + pltpu.roll(marks, 80, 1)
    top = top.reshape(cols, QB, 128)
    factor = jnp.exp(top - jnp.max(top, axis=0, keepdims=True))
    total = jnp.sum(sums.reshape(cols, QB, 128) * factor, axis=0, keepdims=True)
    head = iota((cols, QB, 128), 2) < H
    factor = jnp.where(head, factor / total, 0.0).reshape(count, 128)
    high, low, _ = split(factor)
    wide = dot(high, spread) + dot(low, spread)
    averaged = [
        jnp.sum((tile(t) * wide[:, 128 * t : 128 * (t + 1)]).reshape(cols, QB, 128), axis=0)
        for t in range(4)
    ]
    averaged = jnp.concatenate(averaged, axis=1)

    z = jnp.zeros((RB, CZ), F32)
    for c in range(cols):
        pick = row_of(RB, QB * c)
        mine = (dot(pick, high) + dot(pick, low)) * at_head
        z = z + got[c, :RB].astype(F32) * jnp.sum(mine, axis=1, keepdims=True)
    rows[...] = z

    def mine(k):
        return aux[:, D + k : D + k + 1]

    cut = H * C
    step = H * PV
    shifted = [averaged[:, cut + step * b : cut + step * (b + 1)] - mine(9 + b) for b in range(3)]
    local = [
        mine(a) * shifted[0] + mine(3 + a) * shifted[1] + mine(6 + a) * shifted[2]
        for a in range(3)
    ]
    features = []
    for h in range(H):
        features.append(averaged[:, C * h : C * (h + 1)])
        features += [x[:, PV * h : PV * (h + 1)] for x in local]
        features.append(rows[pl.ds(h, QB, stride=H), :])
    features.append(jnp.zeros((QB, 2 * HALF - H * FEAT), F32))
    features = jnp.concatenate(features, axis=1)
    halves[0], halves[1] = features[:, :HALF], features[:, HALF:]
    core = lax.rem(lax.axis_index("row"), 2)
    mixed = dot(halves[core].astype(BF16), w_mine[...], 1, 1)
    mixed = mixed + dot(halves[1 - core].astype(BF16), w_other[...], 1, 1)
    mixed = aux[:, :D] + mixed
    centred = mixed - jnp.sum(mixed, axis=1, keepdims=True) * (1.0 / D)
    variance = jnp.sum(centred * centred, axis=1, keepdims=True) * (1.0 / D)
    normal = centred * lax.rsqrt(variance + NORM_EPS)
    width = D // cols
    out[...] = jnp.zeros(out.shape, F32)
    for c in range(cols):
        out[c, :, :width] = normal[:, width * c : width * (c + 1)]


def scale_kernel(normal, gain, shift, out):
    width = gain.shape[1]
    y = normal[...][:, :width] * gain[...] + shift[...]
    out[...] = y.T.astype(BF16)


HBM = pl.BlockSpec(memory_space=pltpu.HBM)
VMEM = pl.BlockSpec(memory_space=pltpu.VMEM)
PARAMS = pltpu.CompilerParams(vmem_limit_bytes=VMEM_BYTES)
SMALL_PARAMS = pltpu.CompilerParams(vmem_limit_bytes=16 << 20)


def shape(dims, dtype):
    return jax.ShapeDtypeStruct(dims, dtype)


def held(arrays):
    return [pltpu.VMEM(x.shape, x.dtype) for x in arrays]


def signals(count):
    return pltpu.SemaphoreType.DMA((count,))


def cost(pair, times):
    return pl.CostEstimate(
        flops=2 * times * pair.size * 128, bytes_accessed=2 * times * pair.size, transcendentals=0
    )


def pack(cols, query_single, key_single, key_rotation, key_anchor):
    own = key_single.shape[0]
    return pl.pallas_call(
        pack_kernel,
        in_specs=[HBM] * 4,
        out_specs=[VMEM, VMEM],
        out_shape=[shape((cols,) + query_single.shape, BF16), shape((own, D + 128), BF16)],
        scratch_shapes=held([query_single]) + [pltpu.VMEM((24, own), F32), signals(4)],
        compiler_params=PARAMS,
    )(query_single, key_single, key_rotation, key_anchor)


def key_parts(cols, out_weight, *small):
    keys = small[4].shape[1]
    width = out_weight.shape[0]
    results = [
        shape((cols, width, HALF), BF16),
        shape((DEPTH + WIDE, keys), BF16),
        shape((RB, DEPTH + WIDE), F32),
    ]
    return pl.pallas_call(
        key_kernel,
        in_specs=[HBM] * KEY_SMALL,
        out_specs=[VMEM, HBM, HBM],
        out_shape=results,
        scratch_shapes=held((out_weight,) + small)
        + [pltpu.VMEM((width, 2 * HALF), BF16)]
        + held(results[1:])
        + [pltpu.VMEM((keys, D + 128), BF16), signals(KEY_SMALL), signals(2)],
        compiler_params=pltpu.CompilerParams(vmem_limit_bytes=VMEM_BYTES - 1_000_000),
        cost_estimate=pl.CostEstimate(
            flops=2 * D * keys * 1024, bytes_accessed=16 << 20, transcendentals=0
        ),
    )(out_weight, *small)


def attend(pair, *small):
    blocks, keys = pair.shape[0] // QB, pair.shape[1]
    return pl.pallas_call(
        attend_kernel,
        in_specs=[HBM] * (1 + SMALL),
        out_specs=[VMEM, VMEM],
        out_shape=[shape((blocks, CHUNK, 128), BF16), shape((QB, D + 128), F32)],
        scratch_shapes=held(small)
        + held([pair])
        + [
            pltpu.VMEM((blocks * RB, DEPTH), BF16),
            pltpu.VMEM((blocks * RB, keys), F32),
            pltpu.VMEM((blocks * RB, keys), F32),
            pltpu.VMEM((blocks * RB, keys), BF16),
            pltpu.VMEM((blocks * RB, 128), F32),
            signals(blocks),
            signals(SMALL),
        ],
        compiler_params=PARAMS,
        cost_estimate=cost(pair, 3),
    )(pair, *small)


def finish(cols, *taken):
    return pl.pallas_call(
        lambda *refs: finish_kernel(cols, *refs),
        in_specs=[VMEM] * 4,
        out_specs=VMEM,
        out_shape=shape((cols, QB, 128), F32),
        scratch_shapes=[pltpu.VMEM((RB, CZ), F32), pltpu.VMEM((2, QB, HALF), F32)],
        compiler_params=SMALL_PARAMS,
    )(*taken)


def scale(*taken):
    width, queries = taken[1].shape[1], taken[0].shape[0]
    return pl.pallas_call(
        scale_kernel,
        in_specs=[VMEM] * 3,
        out_specs=VMEM,
        out_shape=shape((width, queries), BF16),
        compiler_params=SMALL_PARAMS,
    )(*taken)


def on_device(
    query_single,
    query_rotation,
    query_anchor,
    query_chain,
    key_single,
    key_rotation,
    key_anchor,
    key_chain,
    key_mask,
    pair_tile,
    query_weight,
    query_point_weight,
    key_weight,
    value_weight,
    key_point_weight,
    value_point_weight,
    pair_weight,
    head_gamma,
    chain_gap,
    out_weight,
    norm_gain,
    norm_shift,
):
    cols = lax.axis_size("col")

    def send(x):
        return lax.all_to_all(x, "col", 0, 0)

    q_pack, k_pack = pack(cols, query_single.T.astype(F32), key_single, key_rotation, key_anchor)
    cores = [[2 * x, 2 * x + 1] for x in range(4)]
    k_pack = lax.all_gather(k_pack, "row", axis=0, tiled=True, axis_index_groups=cores)
    k_others = [
        lax.ppermute(k_pack, "row", [(r, (r + 2 * d) % 8) for r in range(8)]) for d in (1, 2, 3)
    ]
    qall = send(q_pack).reshape(D, -1)
    gamma = head_gamma.reshape(1, -1)
    w_pack, key_side, columns = key_parts(
        cols,
        out_weight.T.astype(F32),
        k_pack,
        *k_others,
        key_chain.reshape(1, -1),
        key_weight.T,
        value_weight.T,
        key_point_weight.T,
        value_point_weight.T,
        gamma,
        chain_gap.reshape(1, -1),
    )
    weights = send(w_pack).reshape(D, HALF)
    parts, aux = attend(
        pair_tile,
        pair_weight.T.astype(F32),
        qall,
        query_rotation,
        query_anchor,
        query_chain.reshape(1, -1),
        query_weight.T,
        query_point_weight.T,
        gamma,
        key_mask.reshape(1, -1),
        columns,
        key_side,
    )
    parts, weights = lax.optimization_barrier((parts, weights))
    w_other = lax.ppermute(weights, "row", [(r, r ^ 1) for r in range(8)])
    normal = finish(cols, send(parts), weights, w_other, aux)
    normal = send(normal).reshape(-1, 128)
    return scale(normal, norm_gain.reshape(1, -1), norm_shift.reshape(1, -1)).T


def solution(mesh):
    placed = (
        P("row", "col"),
        P(None, "row"),
        P(None, "row"),
        P("row"),
        P(("col", "row"), None),
        P(None, ("col", "row")),
        P(None, ("col", "row")),
        P("col"),
        P("col"),
        P("row", "col", None),
        P(),
        P(),
        P(),
        P(),
        P(),
        P(),
        P(),
        P(),
        P(),
        P(None, "col"),
        P("col"),
        P("col"),
    )
    return jax.shard_map(
        on_device, mesh=mesh, in_specs=placed, out_specs=P("row", "col"), check_vma=False
    )
```
